128 devices in a mesh: win: 64 (over x, z, y_hi, core), cfg: 2 (over y_lo).
Axes of the slice: x: 4, y: 4 (y_hi: 2, y_lo: 2; y = y_hi * 2 + y_lo), z: 4, core: 2. Of those that a mesh axis runs over, the one named last changes fastest.
Arguments:
- hidden: bfloat16 [2, 65536, 1536], P('cfg', 'win'), may hold values from -36 to 36
- ln_gain: float32 [1536], replicated, may hold values from 0.1 to 1.9
- qkv_weight: bfloat16 [1536, 2304], P('win'), may hold values from -1 to 1
- out_weight: bfloat16 [1536, 768], P('win'), may hold values from -0.4375 to 0.4375
- proj_weight: bfloat16 [1536, 64], replicated, may hold values from -0.15625 to 0.15625
- latent: float32 [32768, 64], P('win'), may hold values from -6 to 6
- conv_in_weight: bfloat16 [7, 64, 1024], replicated, may hold values from -0.25 to 0.25
- snake_in: float32 [1024], replicated, may hold values from 0.5 to 2
- up_weight: bfloat16 [2, 1024, 8, 512], P(None, None, None, 'cfg'), may hold values from -0.125 to 0.125
- snake_mid: float32 [512], replicated, may hold values from 0.5 to 2
- res_weight: bfloat16 [7, 512, 512], replicated, may hold values from -0.09375 to 0.09375
- snake_out: float32 [512], replicated, may hold values from 0.5 to 2
- mix_weight: bfloat16 [512, 512], replicated, may hold values from -0.25 to 0.25
Outputs:
- latent_next: float32 [32768, 64], P('win')
- decoded: bfloat16 [262144, 512], P(('win', 'cfg'))
The draws below stay inside these ranges and needn't reach their ends.
All inputs are finite; a program needn't handle non-finite values.
Results may differ from the reference program's by a relative error of at most 0.025.
Values may be sent and summed in bfloat16 or wider, within the bound.
A program may use at most 128 MiB of HBM per device.

```python
import math
import jax
import jax.numpy as jnp
from jax import lax

D = 1536
NH = 12
HS = 64
LAT = 64
WIN = 1024
OVL = 512
C0 = 1024
C1 = 512
UP = 8
KIN = 7
KRES = 7
HOP = 512
WINDOWS = 64
FRAMES = 32768
N_WIN = 64


def draw_hidden(key, part):
    key = jax.random.fold_in(key, 11)
    noise_key, row_key, column_key = jax.random.split(key, 3)
    total_rows = 2 * WINDOWS * WIN
    row_scale = jnp.exp(jax.random.uniform(row_key, (total_rows, 1), minval=-1.15, maxval=1.15))
    column_scale = jnp.exp(jax.random.uniform(column_key, (1, D), minval=-1.15, maxval=1.15))
    noise_field = jnp.clip(jax.random.normal(noise_key, (total_rows, D)), -3.5, 3.5)
    sampled = noise_field * row_scale * column_scale
    return sampled.reshape(2, WINDOWS * WIN, D).astype(jnp.bfloat16)


def draw_qkv_weight(key, part):
    key = jax.random.fold_in(key, 23)
    base_key = jax.random.fold_in(key, 0)
    head_width = NH * HS
    sampled = jnp.clip(jax.random.normal(base_key, (D, 3 * head_width)), -4.0, 4.0)
    column_gain = jnp.concatenate([jnp.full((2 * head_width,), 1.41, jnp.float32), jnp.ones((head_width,), jnp.float32)])
    weight = sampled * column_gain[None, :] / jnp.sqrt(jnp.float32(D))
    return jnp.clip(weight, -1.0, 1.0).astype(jnp.bfloat16)


def steps_of(stream_key, extent, shards, smallest, high):
    loudness = 1.0
    for position, blocks in shards:
        steps = jax.random.uniform(jax.random.fold_in(jax.random.fold_in(stream_key, 6), position), (blocks,), jnp.float32, smallest / len(shards), high / len(shards))
        loudness = loudness * jnp.repeat(jnp.exp(steps), extent[position] // blocks).reshape((-1,) + (1,) * (len(extent) - 1 - position))
    return loudness


def scatter_about(stream_key, extent, width, reach, shards=(), held_as=jnp.bfloat16):
    factor_of = steps_of(stream_key, extent, shards, -0.22, 0.18) if shards else 1.0
    values = jax.random.normal(stream_key, extent, jnp.float32) * width * factor_of
    return jnp.minimum(jnp.maximum(values, -reach), reach).astype(held_as)


def setup_inputs(seed: int = 0) -> dict:
    arg_keys = jax.random.split(jax.random.key(seed), 14)
    hidden = draw_hidden(jax.random.fold_in(arg_keys[13], 71), 0)
    ln_gain = jnp.clip(1.0 + 0.18 * jax.random.normal(arg_keys[1], (D,), jnp.float32), 0.1, 1.9)
    qkv_weight = draw_qkv_weight(jax.random.fold_in(arg_keys[13], 71), 0)
    out_weight = scatter_about(arg_keys[3], (D, NH * HS), (NH * HS // 4) ** -0.5, 0.4375, ((0, 64),))
    proj_weight = scatter_about(arg_keys[4], (D, LAT), D ** -0.5, 0.15625)
    latent = scatter_about(arg_keys[5], (FRAMES, LAT), 1.0, 6.0, ((0, 64),), jnp.float32)
    conv_in_weight = scatter_about(arg_keys[6], (KIN, LAT, C0), (KIN * LAT) ** -0.5, 0.25)
    snake_in = jnp.clip(jnp.exp(jax.random.uniform(arg_keys[7], (C0,), jnp.float32, math.log(0.5), math.log(2.0))), 0.5, 2.0)
    up_weight = scatter_about(arg_keys[8], (2, C0, UP, C1), (2 * C0) ** -0.5, 0.125, ((3, 2),))
    snake_mid = jnp.clip(jnp.exp(jax.random.uniform(arg_keys[9], (C1,), jnp.float32, math.log(0.5), math.log(2.0))), 0.5, 2.0)
    res_weight = scatter_about(arg_keys[10], (KRES, C1, C1), (KRES * C1) ** -0.5, 0.09375)
    snake_out = jnp.clip(jnp.exp(jax.random.uniform(arg_keys[11], (C1,), jnp.float32, math.log(0.5), math.log(2.0))), 0.5, 2.0)
    mix_weight = scatter_about(arg_keys[12], (C1, C1), C1 ** -0.5, 0.25)
    return dict(hidden=hidden, ln_gain=ln_gain, qkv_weight=qkv_weight, out_weight=out_weight, proj_weight=proj_weight, latent=latent, conv_in_weight=conv_in_weight, snake_in=snake_in, up_weight=up_weight, snake_mid=snake_mid, res_weight=res_weight, snake_out=snake_out, mix_weight=mix_weight)


guide_scale = 5.0
euler_step = -0.1
norm_eps = 1e-05

def layer_norm(widened, ln_gain):
    average = lax.optimization_barrier(jnp.mean(widened, axis=-1, keepdims=True))
    centred = widened - average
    spread = lax.optimization_barrier(jnp.mean(centred * centred, axis=-1, keepdims=True))
    return centred * lax.rsqrt(spread + norm_eps) * ln_gain

def snake(inputs, rates):
    return inputs + jnp.sin(rates * inputs) ** 2 / rates

def window_attention(projected):
    head_width = NH * HS
    length = projected.shape[0]
    queries = projected[:, :head_width].reshape(length, NH, HS).astype(jnp.float32)
    key_rows = projected[:, head_width:2 * head_width].reshape(length, NH, HS).astype(jnp.float32)
    values = projected[:, 2 * head_width:].reshape(length, NH, HS).astype(jnp.float32)
    scores = jnp.einsum('qhd,khd->hqk', queries, key_rows) * (1.0 / math.sqrt(HS))
    weights = jax.nn.softmax(scores, axis=-1).astype(jnp.bfloat16)
    attended = jnp.einsum('hqk,khd->qhd', weights.astype(jnp.float32), values)
    return attended.reshape(length, head_width).astype(jnp.bfloat16)

def window_prediction(window_rows, ln_gain, qkv_weight, out_weight, proj_weight):
    widened = window_rows.astype(jnp.float32)
    normed = layer_norm(widened, ln_gain).astype(jnp.bfloat16)
    projected = jnp.dot(normed, qkv_weight, preferred_element_type=jnp.float32).astype(jnp.bfloat16)
    attended = window_attention(projected)
    branch = lax.dot_general(attended, out_weight, (((1,), (1,)), ((), ())), preferred_element_type=jnp.float32)
    residual = (widened + branch).astype(jnp.bfloat16)
    return jnp.dot(residual, proj_weight, preferred_element_type=jnp.float32)

def reference(hidden, ln_gain, qkv_weight, out_weight, proj_weight, latent, conv_in_weight, snake_in, up_weight, snake_mid, res_weight, snake_out, mix_weight):
    stacked = hidden.reshape(2, N_WIN, WIN, D).transpose(1, 0, 2, 3)

    def one_window(branches):
        cond_pred = window_prediction(branches[0], ln_gain, qkv_weight, out_weight, proj_weight)
        free_pred = window_prediction(branches[1], ln_gain, qkv_weight, out_weight, proj_weight)
        return guide_scale * cond_pred + (1.0 - guide_scale) * free_pred
    guided = lax.map(one_window, stacked)
    offsets = jnp.arange(HOP, dtype=jnp.float32)
    rising = jnp.where(offsets < OVL, (offsets + 0.5) / OVL, 1.0)[None, :, None]
    head_rows = guided[:, :HOP]
    tail_rows = jnp.roll(guided[:, HOP:], 1, axis=0)
    tail_rows = jnp.pad(tail_rows, ((0, 0), (0, HOP - OVL), (0, 0)))
    blended = rising * head_rows + (1.0 - rising) * tail_rows
    latent_next = latent + euler_step * blended.reshape(N_WIN * HOP, LAT)
    coarse = latent_next.astype(jnp.bfloat16)
    tap_stack = jnp.concatenate([jnp.roll(coarse, KIN // 2 - offset, axis=0) for offset in range(KIN)], axis=1)
    start_feat = jnp.dot(tap_stack, conv_in_weight.reshape(KIN * LAT, C0), preferred_element_type=jnp.float32)
    lifted = snake(start_feat, snake_in).astype(jnp.bfloat16)
    earlier = jnp.roll(lifted, 1, axis=0)
    blocks = jnp.dot(lifted, up_weight[0].reshape(C0, UP * C1), preferred_element_type=jnp.float32)
    blocks = blocks + jnp.dot(earlier, up_weight[1].reshape(C0, UP * C1), preferred_element_type=jnp.float32)
    upsampled = jnp.roll(blocks.reshape(FRAMES * UP, C1), -(UP // 2), axis=0)
    activated = snake(upsampled, snake_mid).astype(jnp.bfloat16)
    convolved = jnp.zeros((FRAMES * UP, C1), jnp.float32)
    for offset in range(KRES):
        shifted = jnp.roll(activated, KRES // 2 - offset, axis=0)
        convolved = convolved + jnp.dot(shifted, res_weight[offset], preferred_element_type=jnp.float32)
    second = snake(convolved, snake_out).astype(jnp.bfloat16)
    decoded = (upsampled + jnp.dot(second, mix_weight, preferred_element_type=jnp.float32)).astype(jnp.bfloat16)
    return (latent_next, decoded)
```

```python
import math
import jax
import jax.numpy as jnp
from jax import lax
from jax.sharding import PartitionSpec as P
from jax.experimental import pallas as pl
from jax.experimental.pallas import tpu as pltpu

F32 = jnp.float32
BF16 = jnp.bfloat16
SIN_COEF = (9.869524955749512, -32.46514129638672, 42.64342498779297, -29.426273345947266, 10.581298828125)

guide_scale = 5.0
euler_step = -0.1
norm_eps = 1e-05


MESH = pl.DeviceIdType.MESH
CHUNKS = 4


def front_kernel(hid_hbm, gain_ref, qkv_ref, wo_ref, proj_ref, lat_ref, up_hbm,
                 own_out, part_out, prev_out, nxt_out, pp_out, lat_out, u_own, u_oth,
                 hid, normed, first, arrived0, wbuf, qkv, attended, pred, xs, edge, uin, urel,
                 load_sem, s0, r0, gs, gr, ls, lr, us, ur, xsend, xrecv, own_sem):
    win, cfg = lax.axis_index("win"), lax.axis_index("cfg")
    core, hi, z, x = lax.rem(win, 2), lax.rem(win // 2, 2), lax.rem(win // 4, 4), win // 16
    n_win = lax.axis_size("win")

    def at(x, z, hi, core):
        return ((x * 4 + z) * 2 + hi) * 2 + core

    other = 1 - cfg
    sibling = (at(x, z, hi, 1 - core), cfg)
    x_up, x_dn = lax.rem(x + 1, 4), lax.rem(x + 3, 4)
    z_up, z_dn = lax.rem(z + 1, 4), lax.rem(z + 3, 4)
    across = [(at(x, z, 1 - hi, 0), other), (at(x, z, 1 - hi, 1), other)]
    facing = (win, other)
    opposite = (at(x, z, 1 - hi, core), other)
    right, left = lax.rem(win + 1, n_win), lax.rem(win + n_win - 1, n_win)
    right2, left2 = lax.rem(win + 2, n_win), lax.rem(win + n_win - 2, n_win)
    to_x_up, to_x_dn = (at(x_up, z, hi, core), cfg), (at(x_dn, z, hi, core), cfg)
    to_z_up, to_z_dn = (at(x, z_up, hi, core), cfg), (at(x, z_dn, hi, core), cfg)

    def remote(src, dst, ssem, rsem, device):
        return pltpu.make_async_remote_copy(src_ref=src, dst_ref=dst, send_sem=ssem, recv_sem=rsem,
                                            device_id=device, device_id_type=MESH)

    def await_in(dst, ssem, rsem):
        remote(dst, dst, ssem, rsem, sibling).wait_recv()

    hid_copy = pltpu.make_async_copy(hid_hbm, hid, load_sem.at[0])
    hid_copy.start()
    uin_copy = pltpu.make_async_copy(up_hbm.at[core], uin, load_sem.at[1])
    uin_copy.start()

    barrier = pltpu.get_barrier_semaphore()
    partners = [sibling, across[0], across[1], to_x_up, to_x_dn, to_z_up, to_z_dn, facing]
    partners += [(w, c) for w in (right, left, right2, left2) for c in (cfg, other)]
    for p in partners:
        pl.semaphore_signal(barrier, inc=1, device_id=p, device_id_type=MESH)

    for c in range(2):
        for i in range(3):
            for part in range(3):
                col = part * 768 + 128 * (2 * i + c)
                first[c, i, 0:24, part * 128:(part + 1) * 128] = qkv_ref[:, col:col + 128]
        first[c, 3, 0:24, :] = wo_ref[:, 384 * c:384 * (c + 1)]
        for i in range(4):
            first[c, i, 24:32, :] = jnp.zeros((8, 384), BF16)
    edge[:, 64:128] = jnp.zeros((32, 64), F32)
    edge[0:16, 0:64] = lat_ref[0:16]
    edge[16:32, 0:64] = lat_ref[496:512]
    pl.semaphore_wait(barrier, len(partners))

    mine = hi * 2 + core
    sends = []

    def go(copy):
        copy.start()
        sends.append(copy)

    go(remote(first.at[1 - core], arrived0.at[mine], s0.at[0], r0.at[mine], sibling))
    for c in range(2):
        go(remote(first.at[c], arrived0.at[mine], s0.at[1 + c], r0.at[mine], across[c]))
    go(remote(edge.at[0:16], lat_out.at[1], ls.at[0], lr.at[1], (left, cfg)))
    go(remote(edge.at[16:32], lat_out.at[0], ls.at[1], lr.at[0], (right, cfg)))

    def views(i):
        a1 = lambda p: wbuf.at[i, core, p, z, 0:48]
        b1 = lambda p: wbuf.at[i, core, x, p, 48:96]
        a2 = lambda r, lo, n: wbuf.at[i, core, pl.ds(lo, n), r, 0:48]
        b2 = lambda r, lo, n: wbuf.at[i, core, r, pl.ds(lo, n), 48:96]
        ring_a = (x, x_up, x_dn, to_x_up, to_x_dn)
        ring_b = (z, z_up, z_dn, to_z_up, to_z_dn)
        return ((a1, a2, ring_a, ring_b, 0), (b1, b2, ring_b, ring_a, 7))

    def stage1(i):
        out = []
        for one, _, (me, up, dn, to_up, to_dn), _, k in views(i):
            out.append(remote(one(me), one(me), gs.at[i, k], gr.at[i, k], to_up))
            out.append(remote(one(me), one(me), gs.at[i, k + 1], gr.at[i, k + 1], to_dn))
        return out

    def stage1_in(i):
        for one, _, (me, up, dn, to_up, to_dn), _, k in views(i):
            await_in(one(dn), gs.at[i, k], gr.at[i, k])
            await_in(one(up), gs.at[i, k + 1], gr.at[i, k + 1])

    def forward1(i):
        return [remote(one(dn), one(dn), gs.at[i, k + 2], gr.at[i, k + 2], to_up)
                for one, _, (me, up, dn, to_up, to_dn), _, k in views(i)]

    def forward1_in(i):
        for one, _, (me, up, dn, to_up, to_dn), _, k in views(i):
            await_in(one(lax.rem(me + 2, 4)), gs.at[i, k + 2], gr.at[i, k + 2])

    def stage2(i):
        out = []
        for _, two, _, (me, up, dn, to_up, to_dn), k in views(i):
            out.append(remote(two(me, 0, 4), two(me, 0, 4), gs.at[i, k + 3], gr.at[i, k + 3], to_up))
            out.append(remote(two(me, 0, 4), two(me, 0, 4), gs.at[i, k + 4], gr.at[i, k + 4], to_dn))
        return out

    def stage2_in(i):
        for _, two, _, (me, up, dn, to_up, to_dn), k in views(i):
            await_in(two(dn, 0, 4), gs.at[i, k + 3], gr.at[i, k + 3])
            await_in(two(up, 0, 4), gs.at[i, k + 4], gr.at[i, k + 4])

    def forward2(i):
        out = []
        for _, two, _, (me, up, dn, to_up, to_dn), k in views(i):
            out.append(remote(two(dn, 0, 2), two(dn, 0, 2), gs.at[i, k + 5], gr.at[i, k + 5], to_up))
            out.append(remote(two(up, 2, 2), two(up, 2, 2), gs.at[i, k + 6], gr.at[i, k + 6], to_dn))
        return out

    def forward2_in(i):
        for _, two, _, (me, up, dn, to_up, to_dn), k in views(i):
            far = lax.rem(me + 2, 4)
            await_in(two(far, 0, 2), gs.at[i, k + 5], gr.at[i, k + 5])
            await_in(two(far, 2, 2), gs.at[i, k + 6], gr.at[i, k + 6])

    def share(i):
        return [remote(wbuf.at[i, core], wbuf.at[i, core], gs.at[i, 14], gr.at[i, 14], sibling)]

    def share_in(i):
        await_in(wbuf.at[i, 1 - core], gs.at[i, 14], gr.at[i, 14])

    def launch(copies):
        for copy in copies:
            copy.start()

    def assemble(i):
        rows = jnp.concatenate([arrived0[p, i].astype(F32)[0:24] for p in range(4)], axis=0)
        wbuf[i, core, x, z] = rows.astype(BF16)

    def norm_rows(b, carry):
        r = pl.ds(pl.multiple_of(b * 128, 128), 128)
        v = hid[r, :].astype(F32)
        centred = v - jnp.mean(v, axis=-1, keepdims=True)
        spread = jnp.mean(centred * centred, axis=-1, keepdims=True)
        normed[r, :] = (centred * lax.rsqrt(spread + norm_eps) * gain_ref[...]).astype(BF16)
        return carry

    def turn_rows(b, carry):
        r = pl.ds(pl.multiple_of(b * 128, 128), 128)
        urel[:, r, :] = jnp.swapaxes(uin[r], 0, 1)
        return carry

    hid_copy.wait()
    lax.fori_loop(0, 4, norm_rows, 0)
    arrived0[mine] = first[core]
    for p in (hi * 2 + 1 - core, (1 - hi) * 2, (1 - hi) * 2 + 1):
        await_in(arrived0.at[p], s0.at[0], r0.at[p])
    assemble(0)
    launch(stage1(0))
    for i in range(1, CHUNKS):
        assemble(i)
    lax.fori_loop(4, 8, norm_rows, 0)
    stage1_in(0)
    launch(forward1(0))
    pred[...] = jnp.dot(hid[...], proj_ref[...], preferred_element_type=F32)
    forward1_in(0)
    launch(stage2(0))
    launch(stage1(1))
    uin_copy.wait()
    lax.fori_loop(0, 4, turn_rows, 0)
    stage2_in(0)
    launch(forward2(0))
    lax.fori_loop(4, 8, turn_rows, 0)

    up_local = pltpu.make_async_copy(urel, u_own.at[:, core], load_sem.at[2])
    up_local.start()
    go(remote(urel, u_own.at[:, core], us.at[0], ur.at[0], sibling))
    go(remote(urel.at[0:4], u_oth.at[0:4, core], us.at[1], ur.at[1], facing))
    go(remote(urel.at[4:8], u_oth.at[4:8, core], us.at[2], ur.at[2], opposite))
    forward2_in(0)
    launch(share(0))
    share_in(0)

    lane_first = lax.broadcasted_iota(jnp.int32, (1, 128), 1) < 64
    one = jnp.ones((), BF16)
    pick = [jnp.where(lane_first, 0.125, 0.0).astype(BF16), jnp.where(lane_first, 0.0, 0.125).astype(BF16)]

    def chunk(i, carry):
        nxt = i + 1
        stage1_in(nxt)
        launch(forward1(nxt))

        def project(b, carry):
            r = pl.ds(pl.multiple_of(b * 256, 256), 256)
            w = jnp.concatenate([wbuf[i, 0].reshape(1536, 384), wbuf[i, 1].reshape(1536, 384)], axis=1)
            res = jnp.dot(normed[r, :], w, preferred_element_type=F32).astype(BF16)
            for g in range(6):
                qkv[g, r, :] = res[:, g * 128:(g + 1) * 128]
            return carry
        lax.fori_loop(0, 4, project, 0)
        forward1_in(nxt)
        launch(stage2(nxt))

        @pl.when(i < 2)
        def _():
            launch(stage1(nxt + 1))

        def heads(c, carry):
            k, v = qkv[3 * c + 1], qkv[3 * c + 2]
            vs = (jnp.where(lane_first, v, one), jnp.where(lane_first, one, v))

            def score(t):
                q = qkv[3 * c, t // 2 * 256:(t // 2 + 1) * 256] * pick[t % 2]
                return lax.dot_general(q, k, (((1,), (1,)), ((), ())), preferred_element_type=F32)
            s, keep = score(0), None
            for t in range(8):
                s_next = score(t + 1) if t < 7 else None
                p = jnp.exp(s - jnp.max(s, axis=-1, keepdims=True)).astype(BF16)
                o = jnp.dot(p, vs[t % 2], preferred_element_type=F32)
                o = o / pltpu.roll(o, 64, 1)
                if t % 2:
                    attended[2 * i + c, t // 2 * 256:(t // 2 + 1) * 256] = jnp.where(lane_first, keep, o).astype(BF16)
                keep, s = o, s_next

            @pl.when(c == 0)
            def _():
                stage2_in(nxt)
                launch(forward2(nxt))
            return carry
        lax.fori_loop(0, 2, heads, 0)
        forward2_in(nxt)
        launch(share(nxt))
        share_in(nxt)
        return carry
    lax.fori_loop(0, 3, chunk, 0)

    factor = jnp.where(cfg == 0, guide_scale, 1.0 - guide_scale).astype(F32)
    wo = jnp.concatenate([wbuf[3, 0].reshape(1536, 384), wbuf[3, 1].reshape(1536, 384)], axis=1)
    folded = lax.dot_general(proj_ref[...], wo, (((0,), (0,)), ((), ())), preferred_element_type=F32).astype(BF16)
    att = jnp.concatenate([attended[g] for g in range(6)], axis=1)
    total = pred[...] + lax.dot_general(att, folded, (((1,), (1,)), ((), ())), preferred_element_type=F32)
    xs[:, 0:64] = (factor * total).astype(BF16)
    xs[:, 64:128] = jnp.zeros((1024, 64), BF16)
    own_copy = pltpu.make_async_copy(xs.at[0:528], own_out, own_sem)
    own_copy.start()
    for c, to in ((0, cfg), (1, other)):
        go(remote(xs.at[496:1024], prev_out.at[cfg], xsend.at[c], xrecv.at[cfg], (right, to)))
        go(remote(xs.at[0:16], nxt_out.at[cfg], xsend.at[2 + c], xrecv.at[2 + cfg], (left, to)))
        go(remote(xs.at[1008:1024], pp_out.at[cfg], xsend.at[4 + c], xrecv.at[4 + cfg], (right2, to)))
    go(remote(xs.at[0:528], part_out, xsend.at[6], xrecv.at[6], facing))

    await_in(u_oth.at[0:4, core], us.at[1], ur.at[1])
    go(remote(u_oth.at[0:4, core], u_oth.at[0:4, core], us.at[3], ur.at[3], sibling))
    await_in(u_oth.at[4:8, core], us.at[2], ur.at[2])
    go(remote(u_oth.at[4:8, core], u_oth.at[4:8, core], us.at[4], ur.at[4], sibling))

    for c in range(2):
        await_in(prev_out.at[c], xsend.at[0], xrecv.at[c])
        await_in(nxt_out.at[c], xsend.at[0], xrecv.at[2 + c])
        await_in(pp_out.at[c], xsend.at[0], xrecv.at[4 + c])
        await_in(lat_out.at[c], ls.at[0], lr.at[c])
    await_in(part_out, xsend.at[6], xrecv.at[6])
    await_in(u_own.at[:, 1 - core], us.at[0], ur.at[0])
    await_in(u_oth.at[0:4, 1 - core], us.at[3], ur.at[3])
    await_in(u_oth.at[4:8, 1 - core], us.at[4], ur.at[4])
    up_local.wait()
    own_copy.wait()
    for copy in sends:
        copy.wait_send()

    def drain(i, carry):
        for copies in (stage1(i), forward1(i), stage2(i), forward2(i), share(i)):
            for copy in copies:
                copy.wait_send()
        return carry
    lax.fori_loop(0, CHUNKS, drain, 0)


def front(hidden, gain, qkv_weight, out_weight, proj_weight, latent, up_weight):
    vm = pl.BlockSpec(memory_space=pltpu.VMEM)
    hbm = pl.BlockSpec(memory_space=pl.ANY)
    dma = pltpu.SemaphoreType.DMA
    shape = jax.ShapeDtypeStruct
    return pl.pallas_call(
        front_kernel,
        out_shape=(shape((528, 128), BF16), shape((528, 128), BF16), shape((2, 528, 128), BF16),
                   shape((2, 16, 128), BF16), shape((2, 16, 128), BF16), shape((2, 16, 128), F32),
                   shape((8, 2, 1024, 256), BF16), shape((8, 2, 1024, 256), BF16)),
        in_specs=[hbm, vm, vm, vm, vm, vm, hbm],
        out_specs=(hbm,) * 8,
        scratch_shapes=[
            pltpu.VMEM((1024, 1536), BF16),
            pltpu.VMEM((1024, 1536), BF16),
            pltpu.VMEM((2, 4, 32, 384), BF16),
            pltpu.VMEM((4, 4, 32, 384), BF16),
            pltpu.VMEM((CHUNKS, 2, 4, 4, 96, 384), BF16),
            pltpu.VMEM((6, 1024, 128), BF16),
            pltpu.VMEM((6, 1024, 128), BF16),
            pltpu.VMEM((1024, 64), F32),
            pltpu.VMEM((1024, 128), BF16),
            pltpu.VMEM((32, 128), F32),
            pltpu.VMEM((1024, 8, 256), BF16),
            pltpu.VMEM((8, 1024, 256), BF16),
            dma((3,)), dma((3,)), dma((4,)), dma((CHUNKS, 15)), dma((CHUNKS, 15)),
            dma((2,)), dma((2,)), dma((5,)), dma((5,)), dma((7,)), dma((7,)), dma,
        ],
        compiler_params=pltpu.CompilerParams(collective_id=0, has_side_effects=True,
                                             vmem_limit_bytes=56 * 1024 * 1024),
        cost_estimate=pl.CostEstimate(flops=14_000_000_000, bytes_accessed=40_000_000, transcendentals=12_600_000),
        name="front",
    )(hidden, gain, qkv_weight, out_weight, proj_weight, latent, up_weight)


def snake(v, scale, inverse):
    t = v * scale
    r = t - jnp.round(t)
    s = r * r
    acc = SIN_COEF[4]
    for c in SIN_COEF[3::-1]:
        acc = acc * s + c
    return v + acc * (s * inverse)


PAD = 16


def decode_kernel(own_ref, part_ref, prev_ref, nxt_ref, pp_ref, halo_ref, lat_ref, cw_ref, a_in_ref, a_mid_ref, a_out_ref,
                  u_own, u_oth, res_hbm, mix_hbm, lat_out, dec_out,
                  ext, lifted, pair, ubuf, act, ups, res, mix, outf, u_sem, w_sem):
    side = lax.axis_index("cfg")
    ucopies = []
    for j in range(8):
        for h, src in ((0, u_own), (1, u_oth)):
            cp = pltpu.make_async_copy(src.at[j], ubuf.at[j, h], u_sem.at[j, h])
            cp.start()
            ucopies.append(cp)
    rcopy = pltpu.make_async_copy(res_hbm, res, w_sem.at[0])
    rcopy.start()
    mcopy = pltpu.make_async_copy(mix_hbm, mix, w_sem.at[1])
    mcopy.start()

    def f32(x):
        return x.astype(F32)
    head = jnp.concatenate([
        f32(prev_ref[0, 0:16]) + f32(prev_ref[1, 0:16]),
        f32(own_ref[0:512]) + f32(part_ref[0:512]),
        f32(nxt_ref[0]) + f32(nxt_ref[1])], axis=0)
    tail = jnp.concatenate([
        f32(pp_ref[0]) + f32(pp_ref[1]),
        f32(prev_ref[0, 16:528]) + f32(prev_ref[1, 16:528]),
        f32(own_ref[512:528]) + f32(part_ref[512:528])], axis=0)
    row = lax.broadcasted_iota(jnp.int32, (544, 128), 0) - PAD
    row = jnp.where(row < 0, row + 512, jnp.where(row >= 512, row - 512, row))
    rising = (row.astype(F32) + 0.5) * (1.0 / 512)
    blended = rising * head + (1.0 - rising) * tail
    extended = jnp.concatenate([halo_ref[0][:, :64], lat_ref[...], halo_ref[1][:, :64]], axis=0)
    nxt_lat = extended + euler_step * blended[:, :64]
    lat_out[...] = nxt_lat[16:528]
    ext[0:544, :] = nxt_lat.astype(BF16).astype(F32)
    ext[544:560, :] = jnp.zeros((16, 64), F32)

    a_in = a_in_ref[...]
    x = ext[pl.ds(pl.multiple_of(side * 256, 256), 296), :]
    acc = None
    for k in range(7):
        d = jnp.dot(x[12 + k:12 + k + 272].astype(BF16), cw_ref[k], preferred_element_type=F32)
        acc = d if acc is None else acc + d
    lifted[...] = snake(acc, a_in * (1 / math.pi), 1.0 / a_in)
    pair[:, 0:1024] = lifted[1:265, :].astype(BF16)
    pair[:, 1024:2048] = lifted[0:264, :].astype(BF16)

    a_mid = a_mid_ref[...]
    mid_scale, mid_inv = a_mid * (1 / math.pi), 1.0 / a_mid
    lhs = pair[...]

    for j in range(8):
        for h in range(2):
            ucopies[2 * j + h].wait()
            cols = pl.multiple_of((side * (1 - 2 * h) + h) * 256, 256)
            outf_blk = jnp.dot(lhs, ubuf[j, h], preferred_element_type=F32)
            lifted[0:264, pl.ds(cols, 256)] = outf_blk
        blk = lifted[0:264, 0:512]
        s = snake(blk, mid_scale, mid_inv)
        if j < 4:
            ups[j + 4] = lifted[1:257, 0:512]
        else:
            ups[j - 4] = blk[0:256]
        act[j] = s[0:256].astype(BF16)
        lifted[0:264, 512:1024] = s
        act[j + 8] = lifted[1:257, 512:1024].astype(BF16)

    rcopy.wait()
    mcopy.wait()
    a_out = a_out_ref[...]
    out_scale, out_inv = a_out * (1 / math.pi), 1.0 / a_out

    def step(i, carry):
        conv = None
        for k in range(7):
            d = jnp.dot(act[i + 1 + k], res[k], preferred_element_type=F32)
            conv = d if conv is None else conv + d
        second = snake(conv, out_scale, out_inv).astype(BF16)
        outf[:, i, :] = ups[i] + jnp.dot(second, mix[...], preferred_element_type=F32)
        return carry
    lax.fori_loop(0, 8, step, 0)
    dec_out[...] = outf[...].reshape(2048, 512).astype(BF16)


def decode_call(own, part, prev, nxt, pp, halo, lat, cw, a_in, a_mid, a_out, u_own, u_oth, res, mix):
    vm = pl.BlockSpec(memory_space=pltpu.VMEM)
    anyspec = pl.BlockSpec(memory_space=pl.ANY)
    return pl.pallas_call(
        decode_kernel,
        out_shape=(jax.ShapeDtypeStruct((512, 64), F32), jax.ShapeDtypeStruct((2048, 512), BF16)),
        in_specs=[vm] * 11 + [anyspec] * 4,
        out_specs=(vm, vm),
        scratch_shapes=[
            pltpu.VMEM((560, 64), F32),
            pltpu.VMEM((272, 1024), F32),
            pltpu.VMEM((264, 2048), BF16),
            pltpu.VMEM((8, 2, 2048, 256), BF16),
            pltpu.VMEM((16, 256, 512), BF16),
            pltpu.VMEM((8, 256, 512), F32),
            pltpu.VMEM((7, 512, 512), BF16),
            pltpu.VMEM((512, 512), BF16),
            pltpu.VMEM((256, 8, 512), F32),
            pltpu.SemaphoreType.DMA((8, 2)),
            pltpu.SemaphoreType.DMA((2,)),
        ],
        compiler_params=pltpu.CompilerParams(vmem_limit_bytes=56 * 1024 * 1024),
        name="decode",
    )(own, part, prev, nxt, pp, halo, lat, cw, a_in, a_mid, a_out, u_own, u_oth, res, mix)


def per_device(hidden, ln_gain, qkv_weight, out_weight, proj_weight, latent, conv_in_weight, snake_in,
               up_weight, snake_mid, res_weight, snake_out, mix_weight):
    own, part, prev, nxt, pp, halo, u_own, u_oth = front(
        hidden[0], ln_gain.reshape(1, -1), qkv_weight, out_weight, proj_weight, latent, up_weight)
    return decode_call(own, part, prev, nxt, pp, halo, latent, conv_in_weight,
                       snake_in.reshape(1, -1), snake_mid.reshape(1, -1), snake_out.reshape(1, -1),
                       u_own.reshape(8, 2048, 256), u_oth.reshape(8, 2048, 256), res_weight, mix_weight)


def solution(mesh):
    in_specs = (
        P("cfg", "win", None),
        P(),
        P("win", None),
        P("win", None),
        P(),
        P("win", None),
        P(),
        P(),
        P(None, None, None, "cfg"),
        P(),
        P(),
        P(),
        P(),
    )
    out_specs = (P("win", None), P(("win", "cfg"), None))
    return jax.shard_map(
        per_device, mesh=mesh, in_specs=in_specs, out_specs=out_specs, check_vma=False
    )
```

```python
import math
import jax
import jax.numpy as jnp
from jax import lax
from jax.sharding import PartitionSpec as P
from jax.experimental import pallas as pl
from jax.experimental.pallas import tpu as pltpu

F32 = jnp.float32
BF16 = jnp.bfloat16
SIN_COEF = (9.869524955749512, -32.46514129638672, 42.64342498779297, -29.426273345947266, 10.581298828125)

guide_scale = 5.0
euler_step = -0.1
norm_eps = 1e-05


MESH = pl.DeviceIdType.MESH
CHUNKS = 4


def front_kernel(hid_hbm, gain_ref, qkv_ref, wo_ref, proj_ref, lat_ref, up_hbm,
                 own_out, part_out, prev_out, nxt_out, pp_out, lat_out, u_own, u_oth,
                 hid, normed, first, arrived0, wbuf, qkv, attended, pred, xs, uin, urel,
                 load_sem, s0, r0, gs, gr, ls, lr, us, ur, xsend, xrecv, own_sem):
    win, cfg = lax.axis_index("win"), lax.axis_index("cfg")
    core, hi, z, x = lax.rem(win, 2), lax.rem(win // 2, 2), lax.rem(win // 4, 4), win // 16
    n_win = lax.axis_size("win")

    def at(x, z, hi, core):
        return ((x * 4 + z) * 2 + hi) * 2 + core

    other = 1 - cfg
    sibling = (at(x, z, hi, 1 - core), cfg)
    x_up, x_dn = lax.rem(x + 1, 4), lax.rem(x + 3, 4)
    z_up, z_dn = lax.rem(z + 1, 4), lax.rem(z + 3, 4)
    across = [(at(x, z, 1 - hi, 0), other), (at(x, z, 1 - hi, 1), other)]
    facing = (win, other)
    opposite = (at(x, z, 1 - hi, core), other)
    right, left = lax.rem(win + 1, n_win), lax.rem(win + n_win - 1, n_win)
    right2, left2 = lax.rem(win + 2, n_win), lax.rem(win + n_win - 2, n_win)
    to_x_up, to_x_dn = (at(x_up, z, hi, core), cfg), (at(x_dn, z, hi, core), cfg)
    to_z_up, to_z_dn = (at(x, z_up, hi, core), cfg), (at(x, z_dn, hi, core), cfg)

    def remote(src, dst, ssem, rsem, device):
        return pltpu.make_async_remote_copy(src_ref=src, dst_ref=dst, send_sem=ssem, recv_sem=rsem,
                                            device_id=device, device_id_type=MESH)

    def await_in(dst, ssem, rsem):
        remote(dst, dst, ssem, rsem, sibling).wait_recv()

    hid_copy = pltpu.make_async_copy(hid_hbm, hid, load_sem.at[0])
    hid_copy.start()
    uin_copy = pltpu.make_async_copy(up_hbm.at[core], uin, load_sem.at[1])
    uin_copy.start()

    barrier = pltpu.get_barrier_semaphore()
    partners = [sibling, across[0], across[1], to_x_up, to_x_dn, to_z_up, to_z_dn, facing]
    partners += [(w, c) for w in (right, left, right2, left2) for c in (cfg, other)]
    for p in partners:
        pl.semaphore_signal(barrier, inc=1, device_id=p, device_id_type=MESH)

    for c in range(2):
        for i in range(3):
            for part in range(3):
                col = part * 768 + 128 * (2 * i + c)
                first[c, i, 0:24, part * 128:(part + 1) * 128] = qkv_ref[:, col:col + 128]
        first[c, 3, 0:24, :] = wo_ref[:, 384 * c:384 * (c + 1)]
        for i in range(4):
            first[c, i, 24:32, :] = jnp.zeros((8, 384), BF16)
    pl.semaphore_wait(barrier, len(partners))

    mine = hi * 2 + core
    sends = []

    def go(copy):
        copy.start()
        sends.append(copy)

    go(remote(first.at[1 - core], arrived0.at[mine], s0.at[0], r0.at[mine], sibling))
    for c in range(2):
        go(remote(first.at[c], arrived0.at[mine], s0.at[1 + c], r0.at[mine], across[c]))
    go(remote(lat_ref.at[:, 0:128], lat_out.at[1], ls.at[0], lr.at[1], (left, cfg)))
    go(remote(lat_ref.at[:, 384:512], lat_out.at[0], ls.at[1], lr.at[0], (right, cfg)))

    def views(i):
        a1 = lambda p: wbuf.at[i, core, p, z, 0:48]
        b1 = lambda p: wbuf.at[i, core, x, p, 48:96]
        a2 = lambda r, lo, n: wbuf.at[i, core, pl.ds(lo, n), r, 0:48]
        b2 = lambda r, lo, n: wbuf.at[i, core, r, pl.ds(lo, n), 48:96]
        ring_a = (x, x_up, x_dn, to_x_up, to_x_dn)
        ring_b = (z, z_up, z_dn, to_z_up, to_z_dn)
        return ((a1, a2, ring_a, ring_b, 0), (b1, b2, ring_b, ring_a, 7))

    def stage1(i):
        out = []
        for one, _, (me, up, dn, to_up, to_dn), _, k in views(i):
            out.append(remote(one(me), one(me), gs.at[i, k], gr.at[i, k], to_up))
            out.append(remote(one(me), one(me), gs.at[i, k + 1], gr.at[i, k + 1], to_dn))
        return out

    def stage1_in(i):
        for one, _, (me, up, dn, to_up, to_dn), _, k in views(i):
            await_in(one(dn), gs.at[i, k], gr.at[i, k])
            await_in(one(up), gs.at[i, k + 1], gr.at[i, k + 1])

    def forward1(i):
        return [remote(one(dn), one(dn), gs.at[i, k + 2], gr.at[i, k + 2], to_up)
                for one, _, (me, up, dn, to_up, to_dn), _, k in views(i)]

    def forward1_in(i):
        for one, _, (me, up, dn, to_up, to_dn), _, k in views(i):
            await_in(one(lax.rem(me + 2, 4)), gs.at[i, k + 2], gr.at[i, k + 2])

    def stage2(i):
        out = []
        for _, two, _, (me, up, dn, to_up, to_dn), k in views(i):
            out.append(remote(two(me, 0, 4), two(me, 0, 4), gs.at[i, k + 3], gr.at[i, k + 3], to_up))
            out.append(remote(two(me, 0, 4), two(me, 0, 4), gs.at[i, k + 4], gr.at[i, k + 4], to_dn))
        return out

    def stage2_in(i):
        for _, two, _, (me, up, dn, to_up, to_dn), k in views(i):
            await_in(two(dn, 0, 4), gs.at[i, k + 3], gr.at[i, k + 3])
            await_in(two(up, 0, 4), gs.at[i, k + 4], gr.at[i, k + 4])

    def forward2(i):
        out = []
        for _, two, _, (me, up, dn, to_up, to_dn), k in views(i):
            out.append(remote(two(dn, 0, 2), two(dn, 0, 2), gs.at[i, k + 5], gr.at[i, k + 5], to_up))
            out.append(remote(two(up, 2, 2), two(up, 2, 2), gs.at[i, k + 6], gr.at[i, k + 6], to_dn))
        return out

    def forward2_in(i):
        for _, two, _, (me, up, dn, to_up, to_dn), k in views(i):
            far = lax.rem(me + 2, 4)
            await_in(two(far, 0, 2), gs.at[i, k + 5], gr.at[i, k + 5])
            await_in(two(far, 2, 2), gs.at[i, k + 6], gr.at[i, k + 6])

    def share(i):
        return [remote(wbuf.at[i, core], wbuf.at[i, core], gs.at[i, 14], gr.at[i, 14], sibling)]

    def share_in(i):
        await_in(wbuf.at[i, 1 - core], gs.at[i, 14], gr.at[i, 14])

    def launch(copies):
        for copy in copies:
            copy.start()

    def assemble(i):
        rows = jnp.concatenate([arrived0[p, i].astype(F32)[0:24] for p in range(4)], axis=0)
        wbuf[i, core, x, z] = rows.astype(BF16)

    gain = gain_ref[...][None, :]

    def norm_rows(b, carry):
        r = pl.ds(pl.multiple_of(b * 128, 128), 128)
        v = hid[r, :].astype(F32)
        centred = v - jnp.mean(v, axis=-1, keepdims=True)
        spread = jnp.mean(centred * centred, axis=-1, keepdims=True)
        normed[r, :] = (centred * lax.rsqrt(spread + norm_eps) * gain).astype(BF16)
        return carry

    def turn_rows(b, carry):
        r = pl.ds(pl.multiple_of(b * 128, 128), 128)
        urel[:, r, :] = jnp.swapaxes(uin[r], 0, 1)
        return carry

    uin_copy.wait()
    lax.fori_loop(0, 8, turn_rows, 0)
    arrived0[mine] = first[core]
    for p in (hi * 2 + 1 - core, (1 - hi) * 2, (1 - hi) * 2 + 1):
        await_in(arrived0.at[p], s0.at[0], r0.at[p])
    assemble(0)
    launch(stage1(0))
    for i in range(1, CHUNKS):
        assemble(i)
        launch(stage1(i))
    for k in range(4):
        go(remote(urel.at[k], u_oth.at[k, core], us.at[k], ur.at[k], facing))
        go(remote(urel.at[4 + k], u_oth.at[4 + k, core], us.at[4 + k], ur.at[4 + k], opposite))
    up_local = pltpu.make_async_copy(urel, u_own.at[:, core], load_sem.at[2])
    up_local.start()
    hid_copy.wait()
    stage1_in(0)
    launch(forward1(0))
    lax.fori_loop(0, 4, norm_rows, 0)
    for i in range(1, CHUNKS):
        stage1_in(i)
        launch(forward1(i))
    forward1_in(0)
    launch(stage2(0))
    forward1_in(1)
    launch(stage2(1))
    lax.fori_loop(4, 8, norm_rows, 0)
    forward1_in(2)
    forward1_in(3)
    stage2_in(0)
    launch(forward2(0))
    launch(stage2(2))
    pred[...] = lax.dot_general(hid[...], proj_ref[...], (((1,), (1,)), ((), ())), preferred_element_type=F32)
    forward2_in(0)
    launch(share(0))
    stage2_in(1)
    launch(forward2(1))
    launch(stage2(3))
    share_in(0)
    go(remote(urel, u_own.at[:, core], us.at[8], ur.at[8], sibling))

    def pass_on(k):
        for q in (k, k + 4):
            piece = u_oth.at[q, core]
            await_in(piece, us.at[q], ur.at[q])
            remote(piece, piece, us.at[9 + q], ur.at[9 + q], sibling).start()

    lane_first = lax.broadcasted_iota(jnp.int32, (1, 128), 1) < 64
    one = jnp.ones((), BF16)
    pick = [jnp.where(lane_first, 0.125, 0.0).astype(BF16), jnp.where(lane_first, 0.0, 0.125).astype(BF16)]

    def chunk(i, carry):
        nxt = i + 1

        def project(b, carry):
            r = pl.ds(pl.multiple_of(b * 256, 256), 256)
            w = jnp.concatenate([wbuf[i, 0].reshape(1536, 384), wbuf[i, 1].reshape(1536, 384)], axis=1)
            res = jnp.dot(normed[r, :], w, preferred_element_type=F32).astype(BF16)
            for g in range(6):
                qkv[g, r, :] = res[:, g * 128:(g + 1) * 128]
            return carry
        lax.fori_loop(0, 4, project, 0)
        forward2_in(nxt)
        launch(share(nxt))

        @pl.when(i == 0)
        def _():
            stage2_in(2)
            launch(forward2(2))

        def heads(c, carry):
            k, v = qkv[3 * c + 1], qkv[3 * c + 2]
            vs = (jnp.where(lane_first, v, one), jnp.where(lane_first, one, v))

            def score(t):
                q = qkv[3 * c, t // 2 * 256:(t // 2 + 1) * 256] * pick[t % 2]
                return lax.dot_general(q, k, (((1,), (1,)), ((), ())), preferred_element_type=F32)
            s, keep = score(0), None
            for t in range(8):
                s_next = score(t + 1) if t < 7 else None
                p = jnp.exp(s - jnp.max(s, axis=-1, keepdims=True)).astype(BF16)
                o = jnp.dot(p, vs[t % 2], preferred_element_type=F32)
                o = o / pltpu.roll(o, 64, 1)
                if t % 2:
                    attended[2 * i + c, t // 2 * 256:(t // 2 + 1) * 256] = jnp.where(lane_first, keep, o).astype(BF16)
                keep, s = o, s_next

            @pl.when((i == 0) & (c == 0))
            def _():
                stage2_in(3)
                launch(forward2(3))
            return carry
        lax.fori_loop(0, 2, heads, 0)
        share_in(nxt)
        pass_on(i)
        return carry
    lax.fori_loop(0, 3, chunk, 0)

    factor = jnp.where(cfg == 0, guide_scale, 1.0 - guide_scale).astype(F32)
    wo = jnp.concatenate([wbuf[3, 0].reshape(1536, 384), wbuf[3, 1].reshape(1536, 384)], axis=1)
    folded = jnp.dot(proj_ref[...], wo, preferred_element_type=F32).astype(BF16)
    att = jnp.concatenate([attended[g] for g in range(6)], axis=1)
    total = pred[...] + lax.dot_general(att, folded, (((1,), (1,)), ((), ())), preferred_element_type=F32)
    xs[:, 0:64] = (factor * total).astype(BF16)
    xs[:, 64:128] = jnp.zeros((1024, 64), BF16)
    own_copy = pltpu.make_async_copy(xs.at[0:528], own_out, own_sem)
    own_copy.start()
    for c, to in ((0, cfg), (1, other)):
        go(remote(xs.at[496:1024], prev_out.at[cfg], xsend.at[c], xrecv.at[cfg], (right, to)))
        go(remote(xs.at[0:16], nxt_out.at[cfg], xsend.at[2 + c], xrecv.at[2 + cfg], (left, to)))
        go(remote(xs.at[1008:1024], pp_out.at[cfg], xsend.at[4 + c], xrecv.at[4 + cfg], (right2, to)))
    go(remote(xs.at[0:528], part_out, xsend.at[6], xrecv.at[6], facing))

    pass_on(3)
    for c in range(2):
        await_in(prev_out.at[c], xsend.at[0], xrecv.at[c])
        await_in(nxt_out.at[c], xsend.at[0], xrecv.at[2 + c])
        await_in(pp_out.at[c], xsend.at[0], xrecv.at[4 + c])
        await_in(lat_out.at[c], ls.at[0], lr.at[c])
    await_in(part_out, xsend.at[6], xrecv.at[6])
    await_in(u_own.at[:, 1 - core], us.at[8], ur.at[8])
    for q in range(8):
        theirs = u_oth.at[q, 1 - core]
        await_in(theirs, us.at[9 + q], ur.at[9 + q])
        piece = u_oth.at[q, core]
        remote(piece, piece, us.at[9 + q], ur.at[9 + q], sibling).wait_send()
    up_local.wait()
    own_copy.wait()
    for copy in sends:
        copy.wait_send()

    def drain(i, carry):
        for copies in (stage1(i), forward1(i), stage2(i), forward2(i), share(i)):
            for copy in copies:
                copy.wait_send()
        return carry
    lax.fori_loop(0, CHUNKS, drain, 0)


def front(hidden, gain, qkv_weight, out_weight, proj_weight, latent, up_weight):
    vm = pl.BlockSpec(memory_space=pltpu.VMEM)
    hbm = pl.BlockSpec(memory_space=pl.ANY)
    dma = pltpu.SemaphoreType.DMA
    shape = jax.ShapeDtypeStruct
    return pl.pallas_call(
        front_kernel,
        out_shape=(shape((528, 128), BF16), shape((528, 128), BF16), shape((2, 528, 128), BF16),
                   shape((2, 16, 128), BF16), shape((2, 16, 128), BF16), shape((2, 64, 128), F32),
                   shape((8, 2, 1024, 256), BF16), shape((8, 2, 1024, 256), BF16)),
        in_specs=[hbm, vm, vm, vm, vm, vm, hbm],
        out_specs=(hbm,) * 8,
        scratch_shapes=[
            pltpu.VMEM((1024, 1536), BF16),
            pltpu.VMEM((1024, 1536), BF16),
            pltpu.VMEM((2, 4, 32, 384), BF16),
            pltpu.VMEM((4, 4, 32, 384), BF16),
            pltpu.VMEM((CHUNKS, 2, 4, 4, 96, 384), BF16),
            pltpu.VMEM((6, 1024, 128), BF16),
            pltpu.VMEM((6, 1024, 128), BF16),
            pltpu.VMEM((1024, 64), F32),
            pltpu.VMEM((1024, 128), BF16),
            pltpu.VMEM((1024, 8, 256), BF16),
            pltpu.VMEM((8, 1024, 256), BF16),
            dma((3,)), dma((3,)), dma((4,)), dma((CHUNKS, 15)), dma((CHUNKS, 15)),
            dma((2,)), dma((2,)), dma((17,)), dma((17,)), dma((7,)), dma((7,)), dma,
        ],
        compiler_params=pltpu.CompilerParams(collective_id=0, has_side_effects=True,
                                             vmem_limit_bytes=56 * 1024 * 1024),
        cost_estimate=pl.CostEstimate(flops=14_000_000_000, bytes_accessed=40_000_000, transcendentals=12_600_000),
        name="front",
    )(hidden, gain, qkv_weight, out_weight, proj_weight, latent, up_weight)


def snake(v, scale, inverse):
    t = v * scale
    r = t - jnp.round(t)
    s = r * r
    acc = SIN_COEF[4]
    for c in SIN_COEF[3::-1]:
        acc = acc * s + c
    return v + acc * (s * inverse)


PAD = 16


def decode_kernel(own_ref, part_ref, prev_ref, nxt_ref, pp_ref, halo_ref, lat_ref, cw_ref, a_in_ref, a_mid_ref, a_out_ref,
                  u_own, u_oth, res_hbm, mix_hbm, lat_out, dec_out,
                  ext, lifted, pair, ubuf, act, ups, res, mix, outf, u_sem, w_sem):
    side = lax.axis_index("cfg")
    ucopies = []
    for j in range(8):
        for h, src in ((0, u_own), (1, u_oth)):
            cp = pltpu.make_async_copy(src.at[j], ubuf.at[j, h], u_sem.at[j, h])
            cp.start()
            ucopies.append(cp)
    rcopy = pltpu.make_async_copy(res_hbm, res, w_sem.at[0])
    rcopy.start()
    mcopy = pltpu.make_async_copy(mix_hbm, mix, w_sem.at[1])
    mcopy.start()

    def f32(x):
        return x.astype(F32)
    head = jnp.concatenate([
        f32(prev_ref[0, 0:16]) + f32(prev_ref[1, 0:16]),
        f32(own_ref[0:512]) + f32(part_ref[0:512]),
        f32(nxt_ref[0]) + f32(nxt_ref[1])], axis=0)
    tail = jnp.concatenate([
        f32(pp_ref[0]) + f32(pp_ref[1]),
        f32(prev_ref[0, 16:528]) + f32(prev_ref[1, 16:528]),
        f32(own_ref[512:528]) + f32(part_ref[512:528])], axis=0)
    row = lax.broadcasted_iota(jnp.int32, (544, 128), 0) - PAD
    row = jnp.where(row < 0, row + 512, jnp.where(row >= 512, row - 512, row))
    rising = (row.astype(F32) + 0.5) * (1.0 / 512)
    blended = rising * head + (1.0 - rising) * tail
    extended = jnp.concatenate([halo_ref[0].T[112:], lat_ref[...].T, halo_ref[1].T[:16]], axis=0)
    nxt_lat = extended + euler_step * blended[:, :64]
    lat_out[...] = nxt_lat[16:528].T
    ext[0:544, :] = nxt_lat.astype(BF16).astype(F32)
    ext[544:560, :] = jnp.zeros((16, 64), F32)

    a_in = a_in_ref[...]
    x = ext[pl.ds(pl.multiple_of(side * 256, 256), 296), :]
    acc = None
    for k in range(7):
        d = jnp.dot(x[12 + k:12 + k + 272].astype(BF16), cw_ref[k], preferred_element_type=F32)
        acc = d if acc is None else acc + d
    lifted[...] = snake(acc, a_in * (1 / math.pi), 1.0 / a_in)
    pair[:, 0:1024] = lifted[1:265, :].astype(BF16)
    pair[:, 1024:2048] = lifted[0:264, :].astype(BF16)

    a_mid = a_mid_ref[...]
    mid_scale, mid_inv = a_mid * (1 / math.pi), 1.0 / a_mid
    lhs = pair[...]

    for j in range(8):
        for h in range(2):
            ucopies[2 * j + h].wait()
            cols = pl.multiple_of((side * (1 - 2 * h) + h) * 256, 256)
            outf_blk = jnp.dot(lhs, ubuf[j, h], preferred_element_type=F32)
            lifted[0:264, pl.ds(cols, 256)] = outf_blk
        blk = lifted[0:264, 0:512]
        s = snake(blk, mid_scale, mid_inv)
        if j < 4:
            ups[j + 4] = lifted[1:257, 0:512]
        else:
            ups[j - 4] = blk[0:256]
        act[j] = s[0:256].astype(BF16)
        lifted[0:264, 512:1024] = s
        act[j + 8] = lifted[1:257, 512:1024].astype(BF16)

    rcopy.wait()
    mcopy.wait()
    a_out = a_out_ref[...]
    out_scale, out_inv = a_out * (1 / math.pi), 1.0 / a_out

    def step(i, carry):
        conv = None
        for k in range(7):
            d = jnp.dot(act[i + 1 + k], res[k], preferred_element_type=F32)
            conv = d if conv is None else conv + d
        second = snake(conv, out_scale, out_inv).astype(BF16)
        outf[:, i, :] = ups[i] + jnp.dot(second, mix[...], preferred_element_type=F32)
        return carry
    lax.fori_loop(0, 8, step, 0)
    dec_out[...] = outf[...].reshape(2048, 512).astype(BF16)


def decode_call(own, part, prev, nxt, pp, halo, lat, cw, a_in, a_mid, a_out, u_own, u_oth, res, mix):
    vm = pl.BlockSpec(memory_space=pltpu.VMEM)
    anyspec = pl.BlockSpec(memory_space=pl.ANY)
    return pl.pallas_call(
        decode_kernel,
        out_shape=(jax.ShapeDtypeStruct((64, 512), F32), jax.ShapeDtypeStruct((2048, 512), BF16)),
        in_specs=[vm] * 11 + [anyspec] * 4,
        out_specs=(vm, vm),
        scratch_shapes=[
            pltpu.VMEM((560, 64), F32),
            pltpu.VMEM((272, 1024), F32),
            pltpu.VMEM((264, 2048), BF16),
            pltpu.VMEM((8, 2, 2048, 256), BF16),
            pltpu.VMEM((16, 256, 512), BF16),
            pltpu.VMEM((8, 256, 512), F32),
            pltpu.VMEM((7, 512, 512), BF16),
            pltpu.VMEM((512, 512), BF16),
            pltpu.VMEM((256, 8, 512), F32),
            pltpu.SemaphoreType.DMA((8, 2)),
            pltpu.SemaphoreType.DMA((2,)),
        ],
        compiler_params=pltpu.CompilerParams(vmem_limit_bytes=56 * 1024 * 1024),
        name="decode",
    )(own, part, prev, nxt, pp, halo, lat, cw, a_in, a_mid, a_out, u_own, u_oth, res, mix)


def per_device(hidden, ln_gain, qkv_weight, out_weight, proj_weight, latent, conv_in_weight, snake_in,
               up_weight, snake_mid, res_weight, snake_out, mix_weight):
    own, part, prev, nxt, pp, halo, u_own, u_oth = front(
        hidden[0], ln_gain, qkv_weight, out_weight, proj_weight.T, latent.T, up_weight)
    latent_next, decoded = decode_call(own, part, prev, nxt, pp, halo, latent.T, conv_in_weight,
                       snake_in.reshape(1, -1), snake_mid.reshape(1, -1), snake_out.reshape(1, -1),
                       u_own.reshape(8, 2048, 256), u_oth.reshape(8, 2048, 256), res_weight, mix_weight)
    return latent_next.T, decoded


def solution(mesh):
    in_specs = (
        P("cfg", "win", None),
        P(),
        P("win", None),
        P("win", None),
        P(),
        P("win", None),
        P(),
        P(),
        P(None, None, None, "cfg"),
        P(),
        P(),
        P(),
        P(),
    )
    out_specs = (P("win", None), P(("win", "cfg"), None))
    return jax.shard_map(
        per_device, mesh=mesh, in_specs=in_specs, out_specs=out_specs, check_vma=False
    )
```

```python
import math
import jax
import jax.numpy as jnp
from jax import lax
from jax.sharding import PartitionSpec as P
from jax.experimental import pallas as pl
from jax.experimental.pallas import tpu as pltpu

F32 = jnp.float32
BF16 = jnp.bfloat16
SIN_COEF = (9.869524955749512, -32.46514129638672, 42.64342498779297, -29.426273345947266, 10.581298828125)

guide_scale = 5.0
euler_step = -0.1
norm_eps = 1e-05


MESH = pl.DeviceIdType.MESH
CHUNKS = 4


def front_kernel(hid_hbm, gain_ref, qkv_ref, wo_ref, proj_ref, lat_ref, up_hbm,
                 own_out, part_out, prev_out, nxt_out, pp_out, lat_out, u_own, u_oth,
                 hid, normed, first, arrived0, wbuf, qkv, attended, pred, xs, uin, urel,
                 load_sem, s0, r0, gs, gr, ls, lr, us, ur, xsend, xrecv, own_sem):
    win, cfg = lax.axis_index("win"), lax.axis_index("cfg")
    core, hi, z, x = lax.rem(win, 2), lax.rem(win // 2, 2), lax.rem(win // 4, 4), win // 16
    n_win = lax.axis_size("win")

    def at(x, z, hi, core):
        return ((x * 4 + z) * 2 + hi) * 2 + core

    other = 1 - cfg
    sibling = (at(x, z, hi, 1 - core), cfg)
    x_up, x_dn = lax.rem(x + 1, 4), lax.rem(x + 3, 4)
    z_up, z_dn = lax.rem(z + 1, 4), lax.rem(z + 3, 4)
    across = [(at(x, z, 1 - hi, 0), other), (at(x, z, 1 - hi, 1), other)]
    facing = (win, other)
    opposite = (at(x, z, 1 - hi, core), other)
    right, left = lax.rem(win + 1, n_win), lax.rem(win + n_win - 1, n_win)
    right2, left2 = lax.rem(win + 2, n_win), lax.rem(win + n_win - 2, n_win)
    to_x_up, to_x_dn = (at(x_up, z, hi, core), cfg), (at(x_dn, z, hi, core), cfg)
    to_z_up, to_z_dn = (at(x, z_up, hi, core), cfg), (at(x, z_dn, hi, core), cfg)

    def remote(src, dst, ssem, rsem, device):
        return pltpu.make_async_remote_copy(src_ref=src, dst_ref=dst, send_sem=ssem, recv_sem=rsem,
                                            device_id=device, device_id_type=MESH)

    def await_in(dst, ssem, rsem):
        remote(dst, dst, ssem, rsem, sibling).wait_recv()

    hid_copy = pltpu.make_async_copy(hid_hbm, hid, load_sem.at[0])
    hid_copy.start()
    uin_copy = pltpu.make_async_copy(up_hbm.at[core], uin, load_sem.at[1])
    uin_copy.start()

    barrier = pltpu.get_barrier_semaphore()
    partners = [sibling, across[0], across[1], to_x_up, to_x_dn, to_z_up, to_z_dn, facing]
    partners += [(w, c) for w in (right, left, right2, left2) for c in (cfg, other)]
    for p in partners:
        pl.semaphore_signal(barrier, inc=1, device_id=p, device_id_type=MESH)

    for c in range(2):
        for i in range(3):
            for part in range(3):
                col = part * 768 + 128 * (2 * i + c)
                first[c, i, 0:24, part * 128:(part + 1) * 128] = qkv_ref[:, col:col + 128]
        first[c, 3, 0:24, :] = wo_ref[:, 384 * c:384 * (c + 1)]
        for i in range(4):
            first[c, i, 24:32, :] = jnp.zeros((8, 384), BF16)
    pl.semaphore_wait(barrier, len(partners))

    mine = hi * 2 + core
    sends = []

    def go(copy):
        copy.start()
        sends.append(copy)

    go(remote(first.at[1 - core], arrived0.at[mine], s0.at[0], r0.at[mine], sibling))
    for c in range(2):
        go(remote(first.at[c], arrived0.at[mine], s0.at[1 + c], r0.at[mine], across[c]))
    go(remote(lat_ref.at[:, 0:128], lat_out.at[1], ls.at[0], lr.at[1], (left, cfg)))
    go(remote(lat_ref.at[:, 384:512], lat_out.at[0], ls.at[1], lr.at[0], (right, cfg)))

    def views(i):
        a1 = lambda p: wbuf.at[i, core, p, z, 0:48]
        b1 = lambda p: wbuf.at[i, core, x, p, 48:96]
        a2 = lambda r, lo, n: wbuf.at[i, core, pl.ds(lo, n), r, 0:48]
        b2 = lambda r, lo, n: wbuf.at[i, core, r, pl.ds(lo, n), 48:96]
        ring_a = (x, x_up, x_dn, to_x_up, to_x_dn)
        ring_b = (z, z_up, z_dn, to_z_up, to_z_dn)
        return ((a1, a2, ring_a, ring_b, 0), (b1, b2, ring_b, ring_a, 7))

    def stage1(i):
        out = []
        for one, _, (me, up, dn, to_up, to_dn), _, k in views(i):
            out.append(remote(one(me), one(me), gs.at[i, k], gr.at[i, k], to_up))
            out.append(remote(one(me), one(me), gs.at[i, k + 1], gr.at[i, k + 1], to_dn))
        return out

    def stage1_in(i):
        for one, _, (me, up, dn, to_up, to_dn), _, k in views(i):
            await_in(one(dn), gs.at[i, k], gr.at[i, k])
            await_in(one(up), gs.at[i, k + 1], gr.at[i, k + 1])

    def forward1(i):
        return [remote(one(dn), one(dn), gs.at[i, k + 2], gr.at[i, k + 2], to_up)
                for one, _, (me, up, dn, to_up, to_dn), _, k in views(i)]

    def forward1_in(i):
        for one, _, (me, up, dn, to_up, to_dn), _, k in views(i):
            await_in(one(lax.rem(me + 2, 4)), gs.at[i, k + 2], gr.at[i, k + 2])

    def stage2(i):
        out = []
        for _, two, _, (me, up, dn, to_up, to_dn), k in views(i):
            out.append(remote(two(me, 0, 4), two(me, 0, 4), gs.at[i, k + 3], gr.at[i, k + 3], to_up))
            out.append(remote(two(me, 0, 4), two(me, 0, 4), gs.at[i, k + 4], gr.at[i, k + 4], to_dn))
        return out

    def stage2_in(i):
        for _, two, _, (me, up, dn, to_up, to_dn), k in views(i):
            await_in(two(dn, 0, 4), gs.at[i, k + 3], gr.at[i, k + 3])
            await_in(two(up, 0, 4), gs.at[i, k + 4], gr.at[i, k + 4])

    def forward2(i):
        out = []
        for _, two, _, (me, up, dn, to_up, to_dn), k in views(i):
            out.append(remote(two(dn, 0, 2), two(dn, 0, 2), gs.at[i, k + 5], gr.at[i, k + 5], to_up))
            out.append(remote(two(up, 2, 2), two(up, 2, 2), gs.at[i, k + 6], gr.at[i, k + 6], to_dn))
        return out

    def forward2_in(i):
        for _, two, _, (me, up, dn, to_up, to_dn), k in views(i):
            far = lax.rem(me + 2, 4)
            await_in(two(far, 0, 2), gs.at[i, k + 5], gr.at[i, k + 5])
            await_in(two(far, 2, 2), gs.at[i, k + 6], gr.at[i, k + 6])

    def share(i):
        return [remote(wbuf.at[i, core], wbuf.at[i, core], gs.at[i, 14], gr.at[i, 14], sibling)]

    def share_in(i):
        await_in(wbuf.at[i, 1 - core], gs.at[i, 14], gr.at[i, 14])

    def launch(copies):
        for copy in copies:
            copy.start()

    def assemble(i):
        rows = jnp.concatenate([arrived0[p, i].astype(F32)[0:24] for p in range(4)], axis=0)
        wbuf[i, core, x, z] = rows.astype(BF16)

    gain = gain_ref[...][None, :]

    def norm_rows(b, carry):
        r = pl.ds(pl.multiple_of(b * 128, 128), 128)
        v = hid[r, :].astype(F32)
        centred = v - jnp.mean(v, axis=-1, keepdims=True)
        spread = jnp.mean(centred * centred, axis=-1, keepdims=True)
        normed[r, :] = (centred * lax.rsqrt(spread + norm_eps) * gain).astype(BF16)
        return carry

    def turn_rows(b, carry):
        r = pl.ds(pl.multiple_of(b * 128, 128), 128)
        urel[:, r, :] = jnp.swapaxes(uin[r], 0, 1)
        return carry

    uin_copy.wait()
    lax.fori_loop(0, 8, turn_rows, 0)
    arrived0[mine] = first[core]
    for p in (hi * 2 + 1 - core, (1 - hi) * 2, (1 - hi) * 2 + 1):
        await_in(arrived0.at[p], s0.at[0], r0.at[p])
    assemble(0)
    launch(stage1(0))
    for i in range(1, CHUNKS):
        assemble(i)
        launch(stage1(i))
    for k in range(4):
        go(remote(urel.at[k], u_oth.at[k, core], us.at[k], ur.at[k], facing))
        go(remote(urel.at[4 + k], u_oth.at[4 + k, core], us.at[4 + k], ur.at[4 + k], opposite))
    up_local = pltpu.make_async_copy(urel, u_own.at[:, core], load_sem.at[2])
    up_local.start()
    hid_copy.wait()
    stage1_in(0)
    launch(forward1(0))
    lax.fori_loop(0, 4, norm_rows, 0)
    for i in range(1, CHUNKS):
        stage1_in(i)
        launch(forward1(i))
    forward1_in(0)
    launch(stage2(0))
    forward1_in(1)
    launch(stage2(1))
    lax.fori_loop(4, 8, norm_rows, 0)
    forward1_in(2)
    forward1_in(3)
    stage2_in(0)
    launch(forward2(0))
    launch(stage2(2))
    pred[...] = lax.dot_general(hid[...], proj_ref[...], (((1,), (1,)), ((), ())), preferred_element_type=F32)
    forward2_in(0)
    launch(share(0))
    stage2_in(1)
    launch(forward2(1))
    launch(stage2(3))
    share_in(0)
    go(remote(urel, u_own.at[:, core], us.at[8], ur.at[8], sibling))

    def pass_on(k):
        for q in (k, k + 4):
            piece = u_oth.at[q, core]
            await_in(piece, us.at[q], ur.at[q])
            remote(piece, piece, us.at[9 + q], ur.at[9 + q], sibling).start()

    lane_first = lax.broadcasted_iota(jnp.int32, (1, 128), 1) < 64
    one = jnp.ones((), BF16)
    pick = [jnp.where(lane_first, 0.125, 0.0).astype(BF16), jnp.where(lane_first, 0.0, 0.125).astype(BF16)]

    def chunk(i, carry):
        nxt = i + 1

        w = jnp.concatenate([wbuf[i, 0].reshape(1536, 384), wbuf[i, 1].reshape(1536, 384)], axis=1)
        res = jnp.dot(normed[...], w, preferred_element_type=F32).astype(BF16)
        for g in range(6):
            qkv[g] = res[:, g * 128:(g + 1) * 128]
        forward2_in(nxt)
        launch(share(nxt))

        @pl.when(i == 0)
        def _():
            stage2_in(2)
            launch(forward2(2))

        def heads(c, carry):
            k, v = qkv[3 * c + 1], qkv[3 * c + 2]
            vs = (jnp.where(lane_first, v, one), jnp.where(lane_first, one, v))

            def score(t):
                q = qkv[3 * c, t // 2 * 256:(t // 2 + 1) * 256] * pick[t % 2]
                return lax.dot_general(q, k, (((1,), (1,)), ((), ())), preferred_element_type=F32)
            s, keep = score(0), None
            for t in range(8):
                s_next = score(t + 1) if t < 7 else None
                p = jnp.exp(s - jnp.max(s, axis=-1, keepdims=True)).astype(BF16)
                o = jnp.dot(p, vs[t % 2], preferred_element_type=F32)
                o = o / pltpu.roll(o, 64, 1)
                if t % 2:
                    attended[2 * i + c, t // 2 * 256:(t // 2 + 1) * 256] = jnp.where(lane_first, keep, o).astype(BF16)
                keep, s = o, s_next

            @pl.when((i == 0) & (c == 0))
            def _():
                stage2_in(3)
                launch(forward2(3))
            return carry
        lax.fori_loop(0, 2, heads, 0)
        share_in(nxt)
        pass_on(i)
        return carry
    lax.fori_loop(0, 3, chunk, 0)

    factor = jnp.where(cfg == 0, guide_scale, 1.0 - guide_scale).astype(F32)
    wo = jnp.concatenate([wbuf[3, 0].reshape(1536, 384), wbuf[3, 1].reshape(1536, 384)], axis=1)
    folded = jnp.dot(proj_ref[...], wo, preferred_element_type=F32).astype(BF16)
    att = jnp.concatenate([attended[g] for g in range(6)], axis=1)
    total = pred[...] + lax.dot_general(att, folded, (((1,), (1,)), ((), ())), preferred_element_type=F32)
    xs[:, 0:64] = (factor * total).astype(BF16)
    xs[:, 64:128] = jnp.zeros((1024, 64), BF16)
    own_copy = pltpu.make_async_copy(xs.at[0:528], own_out, own_sem)
    own_copy.start()
    for c, to in ((0, cfg), (1, other)):
        go(remote(xs.at[496:1024], prev_out.at[cfg], xsend.at[c], xrecv.at[cfg], (right, to)))
        go(remote(xs.at[0:16], nxt_out.at[cfg], xsend.at[2 + c], xrecv.at[2 + cfg], (left, to)))
        go(remote(xs.at[1008:1024], pp_out.at[cfg], xsend.at[4 + c], xrecv.at[4 + cfg], (right2, to)))
    go(remote(xs.at[0:528], part_out, xsend.at[6], xrecv.at[6], facing))

    pass_on(3)
    for c in range(2):
        await_in(prev_out.at[c], xsend.at[0], xrecv.at[c])
        await_in(nxt_out.at[c], xsend.at[0], xrecv.at[2 + c])
        await_in(pp_out.at[c], xsend.at[0], xrecv.at[4 + c])
        await_in(lat_out.at[c], ls.at[0], lr.at[c])
    await_in(part_out, xsend.at[6], xrecv.at[6])
    await_in(u_own.at[:, 1 - core], us.at[8], ur.at[8])
    for q in range(8):
        theirs = u_oth.at[q, 1 - core]
        await_in(theirs, us.at[9 + q], ur.at[9 + q])
        piece = u_oth.at[q, core]
        remote(piece, piece, us.at[9 + q], ur.at[9 + q], sibling).wait_send()
    up_local.wait()
    own_copy.wait()
    for copy in sends:
        copy.wait_send()

    def drain(i, carry):
        for copies in (stage1(i), forward1(i), stage2(i), forward2(i), share(i)):
            for copy in copies:
                copy.wait_send()
        return carry
    lax.fori_loop(0, CHUNKS, drain, 0)


def front(hidden, gain, qkv_weight, out_weight, proj_weight, latent, up_weight):
    vm = pl.BlockSpec(memory_space=pltpu.VMEM)
    hbm = pl.BlockSpec(memory_space=pl.ANY)
    dma = pltpu.SemaphoreType.DMA
    shape = jax.ShapeDtypeStruct
    return pl.pallas_call(
        front_kernel,
        out_shape=(shape((528, 128), BF16), shape((528, 128), BF16), shape((2, 528, 128), BF16),
                   shape((2, 16, 128), BF16), shape((2, 16, 128), BF16), shape((2, 64, 128), F32),
                   shape((8, 2, 1024, 256), BF16), shape((8, 2, 1024, 256), BF16)),
        in_specs=[hbm, vm, vm, vm, vm, vm, hbm],
        out_specs=(hbm,) * 8,
        scratch_shapes=[
            pltpu.VMEM((1024, 1536), BF16),
            pltpu.VMEM((1024, 1536), BF16),
            pltpu.VMEM((2, 4, 32, 384), BF16),
            pltpu.VMEM((4, 4, 32, 384), BF16),
            pltpu.VMEM((CHUNKS, 2, 4, 4, 96, 384), BF16),
            pltpu.VMEM((6, 1024, 128), BF16),
            pltpu.VMEM((6, 1024, 128), BF16),
            pltpu.VMEM((1024, 64), F32),
            pltpu.VMEM((1024, 128), BF16),
            pltpu.VMEM((1024, 8, 256), BF16),
            pltpu.VMEM((8, 1024, 256), BF16),
            dma((3,)), dma((3,)), dma((4,)), dma((CHUNKS, 15)), dma((CHUNKS, 15)),
            dma((2,)), dma((2,)), dma((17,)), dma((17,)), dma((7,)), dma((7,)), dma,
        ],
        compiler_params=pltpu.CompilerParams(collective_id=0, has_side_effects=True,
                                             vmem_limit_bytes=56 * 1024 * 1024),
        cost_estimate=pl.CostEstimate(flops=14_000_000_000, bytes_accessed=40_000_000, transcendentals=12_600_000),
        name="front",
    )(hidden, gain, qkv_weight, out_weight, proj_weight, latent, up_weight)


def snake(v, scale, inverse):
    t = v * scale
    r = t - jnp.round(t)
    s = r * r
    acc = SIN_COEF[4]
    for c in SIN_COEF[3::-1]:
        acc = acc * s + c
    return v + acc * (s * inverse)


PAD = 16


def decode_kernel(own_ref, part_ref, prev_ref, nxt_ref, pp_ref, halo_ref, lat_ref, cw_ref, a_in_ref, a_mid_ref, a_out_ref,
                  u_own, u_oth, res_hbm, mix_hbm, lat_out, dec_out,
                  ext, lifted, pair, ubuf, turned, act, ups, res, mix, outf, u_sem, w_sem):
    side = lax.axis_index("cfg")
    ucopies = []
    for j in range(8):
        for h, src in ((0, u_own), (1, u_oth)):
            cp = pltpu.make_async_copy(src.at[j], ubuf.at[j, h], u_sem.at[j, h])
            cp.start()
            ucopies.append(cp)
    halves = [pl.ds(pl.multiple_of(first * 256, 256), 256) for first in (side, 1 - side)]
    wcopies = []
    for h in range(2):
        wcopies.append(pltpu.make_async_copy(res_hbm.at[:, halves[h]], res.at[:, 256 * h:256 * h + 256], w_sem.at[h]))
        wcopies.append(pltpu.make_async_copy(mix_hbm.at[:, halves[h]], mix.at[:, 256 * h:256 * h + 256], w_sem.at[2 + h]))
    for copy in wcopies:
        copy.start()

    def f32(x):
        return x.astype(F32)
    head = jnp.concatenate([
        f32(prev_ref[0, 0:16]) + f32(prev_ref[1, 0:16]),
        f32(own_ref[0:512]) + f32(part_ref[0:512]),
        f32(nxt_ref[0]) + f32(nxt_ref[1])], axis=0)
    tail = jnp.concatenate([
        f32(pp_ref[0]) + f32(pp_ref[1]),
        f32(prev_ref[0, 16:528]) + f32(prev_ref[1, 16:528]),
        f32(own_ref[512:528]) + f32(part_ref[512:528])], axis=0)
    row = lax.broadcasted_iota(jnp.int32, (544, 128), 0) - PAD
    row = jnp.where(row < 0, row + 512, jnp.where(row >= 512, row - 512, row))
    rising = (row.astype(F32) + 0.5) * (1.0 / 512)
    blended = rising * head + (1.0 - rising) * tail
    extended = jnp.concatenate([halo_ref[0].T[112:], lat_ref[...].T, halo_ref[1].T[:16]], axis=0)
    nxt_lat = extended + euler_step * blended[:, :64]
    lat_out[...] = nxt_lat[16:528].T
    ext[0:544, :] = nxt_lat.astype(BF16).astype(F32)
    ext[544:560, :] = jnp.zeros((16, 64), F32)

    a_in = a_in_ref[...]
    x = ext[pl.ds(pl.multiple_of(side * 256, 256), 296), :]
    acc = None
    for k in range(7):
        d = jnp.dot(x[12 + k:12 + k + 272].astype(BF16), cw_ref[k], preferred_element_type=F32)
        acc = d if acc is None else acc + d
    lifted[...] = snake(acc, a_in * (1 / math.pi), 1.0 / a_in)
    pair[:, 0:1024] = lifted[1:265, :].astype(BF16)
    pair[:, 1024:2048] = lifted[0:264, :].astype(BF16)

    a_mid = jnp.concatenate([a_mid_ref[:, halves[0]], a_mid_ref[:, halves[1]]], axis=1)
    mid_scale, mid_inv = a_mid * (1 / math.pi), 1.0 / a_mid
    lhs = pair[...]

    def raise_two(g):
        for q in range(4):
            ucopies[4 * g + q].wait()
        w = jnp.concatenate([ubuf[2 * g, 0], ubuf[2 * g, 1], ubuf[2 * g + 1, 0], ubuf[2 * g + 1, 1]], axis=1)
        return jnp.dot(lhs, w, preferred_element_type=F32)

    def keep_two(g, both):
        for q in range(2):
            j = 2 * g + q
            blk = both[:, 512 * q:512 * q + 512]
            s = snake(blk, mid_scale, mid_inv)
            act[j] = s[0:256].astype(BF16)
            turned[2 * q + 1] = s
            act[j + 8] = turned[2 * q + 1, 1:257, :].astype(BF16)
            if j < 4:
                turned[2 * q] = blk
                ups[j + 4] = turned[2 * q, 1:257, :]
            else:
                ups[j - 4] = blk[0:256]

    both = raise_two(0)
    for g in range(4):
        later = raise_two(g + 1) if g < 3 else None
        keep_two(g, both)
        both = later

    for copy in wcopies:
        copy.wait()
    a_out = a_out_ref[...]
    out_scale, out_inv = a_out * (1 / math.pi), 1.0 / a_out

    def convolve(i):
        conv = None
        for k in range(7):
            d = jnp.dot(act[2 * i + 1 + k:2 * i + 3 + k].reshape(512, 512), res[k], preferred_element_type=F32)
            conv = d if conv is None else conv + d
        return conv

    def finish(i, conv):
        second = snake(conv, out_scale, out_inv).astype(BF16)
        mixed = jnp.dot(second, mix[...], preferred_element_type=F32)
        for q in range(2):
            outf[:, 2 * i + q, :] = ups[2 * i + q] + mixed[256 * q:256 * q + 256]

    conv = convolve(0)
    for i in range(4):
        later = convolve(i + 1) if i < 3 else None
        finish(i, conv)
        conv = later
    for h in range(2):
        dec_out[:, halves[h]] = outf[:, :, 256 * h:256 * h + 256].reshape(2048, 256).astype(BF16)


def decode_call(own, part, prev, nxt, pp, halo, lat, cw, a_in, a_mid, a_out, u_own, u_oth, res, mix):
    vm = pl.BlockSpec(memory_space=pltpu.VMEM)
    anyspec = pl.BlockSpec(memory_space=pl.ANY)
    return pl.pallas_call(
        decode_kernel,
        out_shape=(jax.ShapeDtypeStruct((64, 512), F32), jax.ShapeDtypeStruct((2048, 512), BF16)),
        in_specs=[vm] * 11 + [anyspec] * 4,
        out_specs=(vm, vm),
        scratch_shapes=[
            pltpu.VMEM((560, 64), F32),
            pltpu.VMEM((272, 1024), F32),
            pltpu.VMEM((264, 2048), BF16),
            pltpu.VMEM((8, 2, 2048, 256), BF16),
            pltpu.VMEM((4, 264, 512), F32),
            pltpu.VMEM((16, 256, 512), BF16),
            pltpu.VMEM((8, 256, 512), F32),
            pltpu.VMEM((7, 512, 512), BF16),
            pltpu.VMEM((512, 512), BF16),
            pltpu.VMEM((256, 8, 512), F32),
            pltpu.SemaphoreType.DMA((8, 2)),
            pltpu.SemaphoreType.DMA((4,)),
        ],
        compiler_params=pltpu.CompilerParams(vmem_limit_bytes=56 * 1024 * 1024),
        name="decode",
    )(own, part, prev, nxt, pp, halo, lat, cw, a_in, a_mid, a_out, u_own, u_oth, res, mix)


def per_device(hidden, ln_gain, qkv_weight, out_weight, proj_weight, latent, conv_in_weight, snake_in,
               up_weight, snake_mid, res_weight, snake_out, mix_weight):
    own, part, prev, nxt, pp, halo, u_own, u_oth = front(
        hidden[0], ln_gain, qkv_weight, out_weight, proj_weight.T, latent.T, up_weight)
    latent_next, decoded = decode_call(own, part, prev, nxt, pp, halo, latent.T, conv_in_weight,
                       snake_in.reshape(1, -1), snake_mid.reshape(1, -1), snake_out.reshape(1, -1),
                       u_own.reshape(8, 2048, 256), u_oth.reshape(8, 2048, 256), res_weight, mix_weight)
    return latent_next.T, decoded


def solution(mesh):
    in_specs = (
        P("cfg", "win", None),
        P(),
        P("win", None),
        P("win", None),
        P(),
        P("win", None),
        P(),
        P(),
        P(None, None, None, "cfg"),
        P(),
        P(),
        P(),
        P(),
    )
    out_specs = (P("win", None), P(("win", "cfg"), None))
    return jax.shard_map(
        per_device, mesh=mesh, in_specs=in_specs, out_specs=out_specs, check_vma=False
    )
```

```python
import math
import jax
import jax.numpy as jnp
from jax import lax
from jax.sharding import PartitionSpec as P
from jax.experimental import pallas as pl
from jax.experimental.pallas import tpu as pltpu

F32 = jnp.float32
BF16 = jnp.bfloat16
SIN_COEF = (9.869524955749512, -32.46514129638672, 42.64342498779297, -29.426273345947266, 10.581298828125)

guide_scale = 5.0
euler_step = -0.1
norm_eps = 1e-05


MESH = pl.DeviceIdType.MESH
CHUNKS = 4


def front_kernel(hid_hbm, gain_ref, qkv_ref, wo_ref, proj_ref, lat_ref, up_hbm,
                 own_out, part_out, prev_out, nxt_out, pp_out, lat_out, u_own, u_oth,
                 hid, normed, first, arrived0, wbuf, qkv, attended, pred, xs, uin, urel,
                 load_sem, s0, r0, gs, gr, ls, lr, us, ur, xsend, xrecv, own_sem):
    win, cfg = lax.axis_index("win"), lax.axis_index("cfg")
    core, hi, z, x = lax.rem(win, 2), lax.rem(win // 2, 2), lax.rem(win // 4, 4), win // 16
    n_win = lax.axis_size("win")

    def at(x, z, hi, core):
        return ((x * 4 + z) * 2 + hi) * 2 + core

    other = 1 - cfg
    sibling = (at(x, z, hi, 1 - core), cfg)
    x_up, x_dn = lax.rem(x + 1, 4), lax.rem(x + 3, 4)
    z_up, z_dn = lax.rem(z + 1, 4), lax.rem(z + 3, 4)
    across = [(at(x, z, 1 - hi, 0), other), (at(x, z, 1 - hi, 1), other)]
    facing = (win, other)
    opposite = (at(x, z, 1 - hi, core), other)
    right, left = lax.rem(win + 1, n_win), lax.rem(win + n_win - 1, n_win)
    right2, left2 = lax.rem(win + 2, n_win), lax.rem(win + n_win - 2, n_win)
    to_x_up, to_x_dn = (at(x_up, z, hi, core), cfg), (at(x_dn, z, hi, core), cfg)
    to_z_up, to_z_dn = (at(x, z_up, hi, core), cfg), (at(x, z_dn, hi, core), cfg)

    def remote(src, dst, ssem, rsem, device):
        return pltpu.make_async_remote_copy(src_ref=src, dst_ref=dst, send_sem=ssem, recv_sem=rsem,
                                            device_id=device, device_id_type=MESH)

    def await_in(dst, ssem, rsem):
        remote(dst, dst, ssem, rsem, sibling).wait_recv()

    hid_copy = pltpu.make_async_copy(hid_hbm, hid, load_sem.at[0])
    hid_copy.start()
    uin_copy = pltpu.make_async_copy(up_hbm.at[core], uin, load_sem.at[1])
    uin_copy.start()

    barrier = pltpu.get_barrier_semaphore()
    partners = [sibling, across[0], across[1], to_x_up, to_x_dn, to_z_up, to_z_dn, facing]
    partners += [(w, c) for w in (right, left, right2, left2) for c in (cfg, other)]
    for p in partners:
        pl.semaphore_signal(barrier, inc=1, device_id=p, device_id_type=MESH)

    for c in range(2):
        for i in range(3):
            for part in range(3):
                col = part * 768 + 128 * (2 * i + c)
                first[c, i, 0:24, part * 128:(part + 1) * 128] = qkv_ref[:, col:col + 128]
        first[c, 3, 0:24, :] = wo_ref[:, 384 * c:384 * (c + 1)]
        for i in range(4):
            first[c, i, 24:32, :] = jnp.zeros((8, 384), BF16)
    pl.semaphore_wait(barrier, len(partners))

    mine = hi * 2 + core
    sends = []

    def go(copy):
        copy.start()
        sends.append(copy)

    go(remote(first.at[1 - core], arrived0.at[mine], s0.at[0], r0.at[mine], sibling))
    for c in range(2):
        go(remote(first.at[c], arrived0.at[mine], s0.at[1 + c], r0.at[mine], across[c]))
    go(remote(lat_ref.at[:, 0:128], lat_out.at[1], ls.at[0], lr.at[1], (left, cfg)))
    go(remote(lat_ref.at[:, 384:512], lat_out.at[0], ls.at[1], lr.at[0], (right, cfg)))

    def views(i):
        a1 = lambda p: wbuf.at[i, core, p, z, 0:48]
        b1 = lambda p: wbuf.at[i, core, x, p, 48:96]
        a2 = lambda r, lo, n: wbuf.at[i, core, pl.ds(lo, n), r, 0:48]
        b2 = lambda r, lo, n: wbuf.at[i, core, r, pl.ds(lo, n), 48:96]
        ring_a = (x, x_up, x_dn, to_x_up, to_x_dn)
        ring_b = (z, z_up, z_dn, to_z_up, to_z_dn)
        return ((a1, a2, ring_a, ring_b, 0), (b1, b2, ring_b, ring_a, 7))

    def stage1(i):
        out = []
        for one, _, (me, up, dn, to_up, to_dn), _, k in views(i):
            out.append(remote(one(me), one(me), gs.at[i, k], gr.at[i, k], to_up))
            out.append(remote(one(me), one(me), gs.at[i, k + 1], gr.at[i, k + 1], to_dn))
        return out

    def stage1_in(i):
        for one, _, (me, up, dn, to_up, to_dn), _, k in views(i):
            await_in(one(dn), gs.at[i, k], gr.at[i, k])
            await_in(one(up), gs.at[i, k + 1], gr.at[i, k + 1])

    def forward1(i):
        return [remote(one(dn), one(dn), gs.at[i, k + 2], gr.at[i, k + 2], to_up)
                for one, _, (me, up, dn, to_up, to_dn), _, k in views(i)]

    def forward1_in(i):
        for one, _, (me, up, dn, to_up, to_dn), _, k in views(i):
            await_in(one(lax.rem(me + 2, 4)), gs.at[i, k + 2], gr.at[i, k + 2])

    def stage2(i):
        out = []
        for _, two, _, (me, up, dn, to_up, to_dn), k in views(i):
            out.append(remote(two(me, 0, 4), two(me, 0, 4), gs.at[i, k + 3], gr.at[i, k + 3], to_up))
            out.append(remote(two(me, 0, 4), two(me, 0, 4), gs.at[i, k + 4], gr.at[i, k + 4], to_dn))
        return out

    def stage2_in(i):
        for _, two, _, (me, up, dn, to_up, to_dn), k in views(i):
            await_in(two(dn, 0, 4), gs.at[i, k + 3], gr.at[i, k + 3])
            await_in(two(up, 0, 4), gs.at[i, k + 4], gr.at[i, k + 4])

    def forward2(i):
        out = []
        for _, two, _, (me, up, dn, to_up, to_dn), k in views(i):
            out.append(remote(two(dn, 0, 2), two(dn, 0, 2), gs.at[i, k + 5], gr.at[i, k + 5], to_up))
            out.append(remote(two(up, 2, 2), two(up, 2, 2), gs.at[i, k + 6], gr.at[i, k + 6], to_dn))
        return out

    def forward2_in(i):
        for _, two, _, (me, up, dn, to_up, to_dn), k in views(i):
            far = lax.rem(me + 2, 4)
            await_in(two(far, 0, 2), gs.at[i, k + 5], gr.at[i, k + 5])
            await_in(two(far, 2, 2), gs.at[i, k + 6], gr.at[i, k + 6])

    def part(i, carrier, v, r):
        return wbuf.at[i, carrier, pl.ds(0, 4), r, 0:48] if v == 0 else wbuf.at[i, carrier, r, pl.ds(0, 4), 48:96]

    def slots(v):
        return (z, z_up, z_dn, lax.rem(z + 2, 4)) if v == 0 else (x, x_up, x_dn, lax.rem(x + 2, 4))

    def share(i, lo, hi):
        out = []
        for v in range(2):
            for n, r in enumerate(slots(v)[lo:hi], lo):
                k = 14 + 4 * v + n
                out.append(remote(part(i, core, v, r), part(i, core, v, r), gs.at[i, k], gr.at[i, k], sibling))
        return out

    def share_in(i):
        for v in range(2):
            for n, r in enumerate(slots(v)):
                k = 14 + 4 * v + n
                await_in(part(i, 1 - core, v, r), gs.at[i, k], gr.at[i, k])

    def launch(copies):
        for copy in copies:
            copy.start()

    def assemble(i):
        rows = jnp.concatenate([arrived0[p, i].astype(F32)[0:24] for p in range(4)], axis=0)
        wbuf[i, core, x, z] = rows.astype(BF16)

    gain = gain_ref[...][None, :]

    def norm_rows(b, carry):
        r = pl.ds(pl.multiple_of(b * 128, 128), 128)
        v = hid[r, :].astype(F32)
        centred = v - jnp.mean(v, axis=-1, keepdims=True)
        spread = jnp.mean(centred * centred, axis=-1, keepdims=True)
        normed[r, :] = (centred * lax.rsqrt(spread + norm_eps) * gain).astype(BF16)
        return carry

    def turn_rows(b, carry):
        r = pl.ds(pl.multiple_of(b * 128, 128), 128)
        urel[:, r, :] = jnp.swapaxes(uin[r], 0, 1)
        return carry

    uin_copy.wait()
    lax.fori_loop(0, 8, turn_rows, 0)
    arrived0[mine] = first[core]
    for p in (hi * 2 + 1 - core, (1 - hi) * 2, (1 - hi) * 2 + 1):
        await_in(arrived0.at[p], s0.at[0], r0.at[p])
    assemble(0)
    launch(stage1(0))
    for i in range(1, CHUNKS):
        assemble(i)
        launch(stage1(i))
    for k in range(4):
        go(remote(urel.at[k], u_oth.at[k, core], us.at[k], ur.at[k], facing))
        go(remote(urel.at[4 + k], u_oth.at[4 + k, core], us.at[4 + k], ur.at[4 + k], opposite))
    up_local = pltpu.make_async_copy(urel, u_own.at[:, core], load_sem.at[2])
    up_local.start()
    hid_copy.wait()
    stage1_in(0)
    launch(forward1(0))
    lax.fori_loop(0, 4, norm_rows, 0)
    for i in range(1, CHUNKS):
        stage1_in(i)
        launch(forward1(i))
    forward1_in(0)
    launch(stage2(0))
    forward1_in(1)
    launch(stage2(1))
    lax.fori_loop(4, 8, norm_rows, 0)
    forward1_in(2)
    forward1_in(3)
    stage2_in(0)
    launch(forward2(0))
    launch(stage2(2))
    launch(share(0, 0, 3))
    pred[...] = lax.dot_general(hid[...], proj_ref[...], (((1,), (1,)), ((), ())), preferred_element_type=F32)
    forward2_in(0)
    launch(share(0, 3, 4))
    stage2_in(1)
    launch(forward2(1))
    launch(stage2(3))
    share_in(0)
    go(remote(urel, u_own.at[:, core], us.at[8], ur.at[8], sibling))

    def pass_on(k):
        for q in (k, k + 4):
            piece = u_oth.at[q, core]
            await_in(piece, us.at[q], ur.at[q])
            remote(piece, piece, us.at[9 + q], ur.at[9 + q], sibling).start()

    lane_first = lax.broadcasted_iota(jnp.int32, (1, 128), 1) < 64
    one = jnp.ones((), BF16)
    pick = [jnp.where(lane_first, 0.125, 0.0).astype(BF16), jnp.where(lane_first, 0.0, 0.125).astype(BF16)]

    def chunk(i, carry):
        nxt = i + 1

        w = jnp.concatenate([wbuf[i, 0].reshape(1536, 384), wbuf[i, 1].reshape(1536, 384)], axis=1)
        res = jnp.dot(normed[...], w, preferred_element_type=F32).astype(BF16)
        for g in range(6):
            qkv[g] = res[:, g * 128:(g + 1) * 128]
        forward2_in(nxt)
        launch(share(nxt, 0, 4))

        @pl.when(i == 0)
        def _():
            stage2_in(2)
            launch(forward2(2))

        def heads(c, carry):
            k, v = qkv[3 * c + 1], qkv[3 * c + 2]
            vs = (jnp.where(lane_first, v, one), jnp.where(lane_first, one, v))

            def score(t):
                q = qkv[3 * c, t // 2 * 256:(t // 2 + 1) * 256] * pick[t % 2]
                return lax.dot_general(q, k, (((1,), (1,)), ((), ())), preferred_element_type=F32)
            s, keep = score(0), None
            for t in range(8):
                s_next = score(t + 1) if t < 7 else None
                p = jnp.exp(s - jnp.max(s, axis=-1, keepdims=True)).astype(BF16)
                o = jnp.dot(p, vs[t % 2], preferred_element_type=F32)
                o = o / pltpu.roll(o, 64, 1)
                if t % 2:
                    attended[2 * i + c, t // 2 * 256:(t // 2 + 1) * 256] = jnp.where(lane_first, keep, o).astype(BF16)
                keep, s = o, s_next

            @pl.when((i == 0) & (c == 0))
            def _():
                stage2_in(3)
                launch(forward2(3))
            return carry
        lax.fori_loop(0, 2, heads, 0)
        share_in(nxt)
        pass_on(i)
        return carry
    lax.fori_loop(0, 3, chunk, 0)

    factor = jnp.where(cfg == 0, guide_scale, 1.0 - guide_scale).astype(F32)
    wo = jnp.concatenate([wbuf[3, 0].reshape(1536, 384), wbuf[3, 1].reshape(1536, 384)], axis=1)
    folded = jnp.dot(proj_ref[...], wo, preferred_element_type=F32).astype(BF16)
    att = jnp.concatenate([attended[g] for g in range(6)], axis=1)
    total = pred[...] + lax.dot_general(att, folded, (((1,), (1,)), ((), ())), preferred_element_type=F32)
    xs[:, 0:64] = (factor * total).astype(BF16)
    xs[:, 64:128] = jnp.zeros((1024, 64), BF16)
    own_copy = pltpu.make_async_copy(xs.at[0:528], own_out, own_sem)
    own_copy.start()
    for c, to in ((0, cfg), (1, other)):
        go(remote(xs.at[496:1024], prev_out.at[cfg], xsend.at[c], xrecv.at[cfg], (right, to)))
        go(remote(xs.at[0:16], nxt_out.at[cfg], xsend.at[2 + c], xrecv.at[2 + cfg], (left, to)))
        go(remote(xs.at[1008:1024], pp_out.at[cfg], xsend.at[4 + c], xrecv.at[4 + cfg], (right2, to)))
    go(remote(xs.at[0:528], part_out, xsend.at[6], xrecv.at[6], facing))

    pass_on(3)
    for c in range(2):
        await_in(prev_out.at[c], xsend.at[0], xrecv.at[c])
        await_in(nxt_out.at[c], xsend.at[0], xrecv.at[2 + c])
        await_in(pp_out.at[c], xsend.at[0], xrecv.at[4 + c])
        await_in(lat_out.at[c], ls.at[0], lr.at[c])
    await_in(part_out, xsend.at[6], xrecv.at[6])
    await_in(u_own.at[:, 1 - core], us.at[8], ur.at[8])
    for q in range(8):
        theirs = u_oth.at[q, 1 - core]
        await_in(theirs, us.at[9 + q], ur.at[9 + q])
        piece = u_oth.at[q, core]
        remote(piece, piece, us.at[9 + q], ur.at[9 + q], sibling).wait_send()
    up_local.wait()
    own_copy.wait()
    for copy in sends:
        copy.wait_send()

    def drain(i, carry):
        for copies in (stage1(i), forward1(i), stage2(i), forward2(i), share(i, 0, 4)):
            for copy in copies:
                copy.wait_send()
        return carry
    lax.fori_loop(0, CHUNKS, drain, 0)


def front(hidden, gain, qkv_weight, out_weight, proj_weight, latent, up_weight):
    vm = pl.BlockSpec(memory_space=pltpu.VMEM)
    hbm = pl.BlockSpec(memory_space=pl.ANY)
    dma = pltpu.SemaphoreType.DMA
    shape = jax.ShapeDtypeStruct
    return pl.pallas_call(
        front_kernel,
        out_shape=(shape((528, 128), BF16), shape((528, 128), BF16), shape((2, 528, 128), BF16),
                   shape((2, 16, 128), BF16), shape((2, 16, 128), BF16), shape((2, 64, 128), F32),
                   shape((8, 2, 1024, 256), BF16), shape((8, 2, 1024, 256), BF16)),
        in_specs=[hbm, vm, vm, vm, vm, vm, hbm],
        out_specs=(hbm,) * 8,
        scratch_shapes=[
            pltpu.VMEM((1024, 1536), BF16),
            pltpu.VMEM((1024, 1536), BF16),
            pltpu.VMEM((2, 4, 32, 384), BF16),
            pltpu.VMEM((4, 4, 32, 384), BF16),
            pltpu.VMEM((CHUNKS, 2, 4, 4, 96, 384), BF16),
            pltpu.VMEM((6, 1024, 128), BF16),
            pltpu.VMEM((6, 1024, 128), BF16),
            pltpu.VMEM((1024, 64), F32),
            pltpu.VMEM((1024, 128), BF16),
            pltpu.VMEM((1024, 8, 256), BF16),
            pltpu.VMEM((8, 1024, 256), BF16),
            dma((3,)), dma((3,)), dma((4,)), dma((CHUNKS, 22)), dma((CHUNKS, 22)),
            dma((2,)), dma((2,)), dma((17,)), dma((17,)), dma((7,)), dma((7,)), dma,
        ],
        compiler_params=pltpu.CompilerParams(collective_id=0, has_side_effects=True,
                                             vmem_limit_bytes=56 * 1024 * 1024),
        cost_estimate=pl.CostEstimate(flops=14_000_000_000, bytes_accessed=40_000_000, transcendentals=12_600_000),
        name="front",
    )(hidden, gain, qkv_weight, out_weight, proj_weight, latent, up_weight)


def snake(v, scale, inverse):
    t = v * scale
    r = t - jnp.round(t)
    s = r * r
    acc = SIN_COEF[4]
    for c in SIN_COEF[3::-1]:
        acc = acc * s + c
    return v + acc * (s * inverse)


PAD = 16


def decode_kernel(own_ref, part_ref, prev_ref, nxt_ref, pp_ref, halo_ref, lat_ref, cw_ref, a_in_ref, a_mid_ref, a_out_ref,
                  u_own, u_oth, res_hbm, mix_hbm, lat_out, dec_out,
                  ext, lifted, pair, ubuf, turned, act, ups, res, mix, outf, u_sem, w_sem):
    side = lax.axis_index("cfg")
    ucopies = []
    for j in range(8):
        for h, src in ((0, u_own), (1, u_oth)):
            cp = pltpu.make_async_copy(src.at[j], ubuf.at[j, h], u_sem.at[j, h])
            cp.start()
            ucopies.append(cp)
    halves = [pl.ds(pl.multiple_of(first * 256, 256), 256) for first in (side, 1 - side)]
    wcopies = []
    for h in range(2):
        wcopies.append(pltpu.make_async_copy(res_hbm.at[:, halves[h]], res.at[:, 256 * h:256 * h + 256], w_sem.at[h]))
        wcopies.append(pltpu.make_async_copy(mix_hbm.at[:, halves[h]], mix.at[:, 256 * h:256 * h + 256], w_sem.at[2 + h]))
    for copy in wcopies:
        copy.start()

    def f32(x):
        return x.astype(F32)
    head = jnp.concatenate([
        f32(prev_ref[0, 0:16]) + f32(prev_ref[1, 0:16]),
        f32(own_ref[0:512]) + f32(part_ref[0:512]),
        f32(nxt_ref[0]) + f32(nxt_ref[1])], axis=0)
    tail = jnp.concatenate([
        f32(pp_ref[0]) + f32(pp_ref[1]),
        f32(prev_ref[0, 16:528]) + f32(prev_ref[1, 16:528]),
        f32(own_ref[512:528]) + f32(part_ref[512:528])], axis=0)
    row = lax.broadcasted_iota(jnp.int32, (544, 128), 0) - PAD
    row = jnp.where(row < 0, row + 512, jnp.where(row >= 512, row - 512, row))
    rising = (row.astype(F32) + 0.5) * (1.0 / 512)
    blended = rising * head + (1.0 - rising) * tail
    extended = jnp.concatenate([halo_ref[0].T[112:], lat_ref[...].T, halo_ref[1].T[:16]], axis=0)
    nxt_lat = extended + euler_step * blended[:, :64]
    lat_out[...] = nxt_lat[16:528].T
    ext[0:544, :] = nxt_lat.astype(BF16).astype(F32)
    ext[544:560, :] = jnp.zeros((16, 64), F32)

    a_in = a_in_ref[...]
    x = ext[pl.ds(pl.multiple_of(side * 256, 256), 296), :]
    acc = None
    for k in range(7):
        d = jnp.dot(x[12 + k:12 + k + 272].astype(BF16), cw_ref[k], preferred_element_type=F32)
        acc = d if acc is None else acc + d
    lifted[...] = snake(acc, a_in * (1 / math.pi), 1.0 / a_in)
    pair[:, 0:1024] = lifted[1:265, :].astype(BF16)
    pair[:, 1024:2048] = lifted[0:264, :].astype(BF16)

    a_mid = jnp.concatenate([a_mid_ref[:, halves[0]], a_mid_ref[:, halves[1]]], axis=1)
    mid_scale, mid_inv = a_mid * (1 / math.pi), 1.0 / a_mid
    lhs = pair[...]

    def raise_two(g):
        for q in range(4):
            ucopies[4 * g + q].wait()
        w = jnp.concatenate([ubuf[2 * g, 0], ubuf[2 * g, 1], ubuf[2 * g + 1, 0], ubuf[2 * g + 1, 1]], axis=1)
        return jnp.dot(lhs, w, preferred_element_type=F32)

    def keep_two(g, both):
        for q in range(2):
            j = 2 * g + q
            blk = both[:, 512 * q:512 * q + 512]
            s = snake(blk, mid_scale, mid_inv)
            act[j] = s[0:256].astype(BF16)
            turned[2 * q + 1] = s
            act[j + 8] = turned[2 * q + 1, 1:257, :].astype(BF16)
            if j < 4:
                turned[2 * q] = blk
                ups[j + 4] = turned[2 * q, 1:257, :]
            else:
                ups[j - 4] = blk[0:256]

    both = raise_two(0)
    for g in range(4):
        later = raise_two(g + 1) if g < 3 else None
        keep_two(g, both)
        both = later

    for copy in wcopies:
        copy.wait()
    a_out = a_out_ref[...]
    out_scale, out_inv = a_out * (1 / math.pi), 1.0 / a_out

    def convolve(i):
        conv = None
        for k in range(7):
            d = jnp.dot(act[2 * i + 1 + k:2 * i + 3 + k].reshape(512, 512), res[k], preferred_element_type=F32)
            conv = d if conv is None else conv + d
        return conv

    def finish(i, conv):
        second = snake(conv, out_scale, out_inv).astype(BF16)
        mixed = jnp.dot(second, mix[...], preferred_element_type=F32)
        for q in range(2):
            outf[:, 2 * i + q, :] = ups[2 * i + q] + mixed[256 * q:256 * q + 256]

    conv = convolve(0)
    for i in range(4):
        later = convolve(i + 1) if i < 3 else None
        finish(i, conv)
        conv = later
    for h in range(2):
        dec_out[:, halves[h]] = outf[:, :, 256 * h:256 * h + 256].reshape(2048, 256).astype(BF16)


def decode_call(own, part, prev, nxt, pp, halo, lat, cw, a_in, a_mid, a_out, u_own, u_oth, res, mix):
    vm = pl.BlockSpec(memory_space=pltpu.VMEM)
    anyspec = pl.BlockSpec(memory_space=pl.ANY)
    return pl.pallas_call(
        decode_kernel,
        out_shape=(jax.ShapeDtypeStruct((64, 512), F32), jax.ShapeDtypeStruct((2048, 512), BF16)),
        in_specs=[vm] * 11 + [anyspec] * 4,
        out_specs=(vm, vm),
        scratch_shapes=[
            pltpu.VMEM((560, 64), F32),
            pltpu.VMEM((272, 1024), F32),
            pltpu.VMEM((264, 2048), BF16),
            pltpu.VMEM((8, 2, 2048, 256), BF16),
            pltpu.VMEM((4, 264, 512), F32),
            pltpu.VMEM((16, 256, 512), BF16),
            pltpu.VMEM((8, 256, 512), F32),
            pltpu.VMEM((7, 512, 512), BF16),
            pltpu.VMEM((512, 512), BF16),
            pltpu.VMEM((256, 8, 512), F32),
            pltpu.SemaphoreType.DMA((8, 2)),
            pltpu.SemaphoreType.DMA((4,)),
        ],
        compiler_params=pltpu.CompilerParams(vmem_limit_bytes=56 * 1024 * 1024),
        name="decode",
    )(own, part, prev, nxt, pp, halo, lat, cw, a_in, a_mid, a_out, u_own, u_oth, res, mix)


def per_device(hidden, ln_gain, qkv_weight, out_weight, proj_weight, latent, conv_in_weight, snake_in,
               up_weight, snake_mid, res_weight, snake_out, mix_weight):
    own, part, prev, nxt, pp, halo, u_own, u_oth = front(
        hidden[0], ln_gain, qkv_weight, out_weight, proj_weight.T, latent.T, up_weight)
    latent_next, decoded = decode_call(own, part, prev, nxt, pp, halo, latent.T, conv_in_weight,
                       snake_in.reshape(1, -1), snake_mid.reshape(1, -1), snake_out.reshape(1, -1),
                       u_own.reshape(8, 2048, 256), u_oth.reshape(8, 2048, 256), res_weight, mix_weight)
    return latent_next.T, decoded


def solution(mesh):
    in_specs = (
        P("cfg", "win", None),
        P(),
        P("win", None),
        P("win", None),
        P(),
        P("win", None),
        P(),
        P(),
        P(None, None, None, "cfg"),
        P(),
        P(),
        P(),
        P(),
    )
    out_specs = (P("win", None), P(("win", "cfg"), None))
    return jax.shard_map(
        per_device, mesh=mesh, in_specs=in_specs, out_specs=out_specs, check_vma=False
    )
```
